128 devices in a mesh: outer: 2 (over z_hi), inner: 8 (over z_lo, x), tensor: 8 (over y, core).
Axes of the slice: x: 4, y: 4, z: 4 (z_hi: 2, z_lo: 2; z = z_hi * 2 + z_lo), core: 2. Of those that a mesh axis runs over, the one named last changes fastest.
Arguments:
- queries: bfloat16 [4096, 8192], P(('outer', 'inner'), 'tensor'), may hold values from -64 to 64
- keys: bfloat16 [4096, 1024], P(('outer', 'inner'), 'tensor'), may hold values from -5 to 5
- values: bfloat16 [4096, 1024], P(('outer', 'inner'), 'tensor'), may hold values from -8 to 8
- positions: int32 [4096], replicated, may hold values from 0 to 4095, as said below
- doc_lengths: int32 [8], replicated, may hold values from 1 to 1024, 4096 in all
- image_spans: int32 [2, 4], replicated, may hold values from 0 to 4096, as said below
- out_weight: bfloat16 [8192, 8192], P('tensor', ('outer', 'inner')), may hold values from -0.0625 to 0.0625
Outputs:
- layer_output: bfloat16 [4096, 8192], P(('outer', 'inner'), 'tensor')
The draws below stay inside these ranges and needn't reach their ends.
Inputs may be any that keep to these rules, and one draw needn't show every extreme that they name: A permutation of the slots' positions that keeps each aligned run of 64 slots on 64 consecutive positions, in order. `image_spans`: spans are disjoint and ascending; each holds 1 to 3 whole image tiles of 256 tokens; the first span starts at 0 and the last ends at 4096.
All inputs are finite; a program needn't handle non-finite values.
Results may differ from the reference program's by a relative error of at most 0.019.
Values may be sent and summed in bfloat16 or wider, within the bound.
No kernel may reach another device: no remote copies, remote signals or barrier semaphores. Data moves between devices by JAX's collectives and lax.ppermute only.
A program may use at most 128 MiB of HBM per device.

```python
import math
import jax
import jax.numpy as jnp
import numpy as np
from jax import lax

D = 8192
HQ = 64
KVH = 8
DH = 128
BLOCK = 64
DOCS = 8
IMG_TOK = 256
TOKENS = 4096
SPANS = 4


def key_normal(key):
    return jnp.clip(jax.random.normal(key, (TOKENS, KVH * DH), jnp.float32), -4.5, 4.5)


def draw_keys(key, part):
    base = key_normal(key)
    return base.astype(jnp.bfloat16)


def draw_queries(key, part):
    key = jax.random.fold_in(key, 2)
    base = 2.0 * jnp.clip(jax.random.normal(key, (TOKENS, HQ * DH), jnp.float32), -4.0, 4.0)
    return base.astype(jnp.bfloat16)


def draw_positions(key, part):
    key = jax.random.fold_in(key, 3)
    order = jax.random.permutation(key, TOKENS // BLOCK).astype(jnp.int32)
    slots = jnp.arange(TOKENS, dtype=jnp.int32)
    return (order[slots // BLOCK] * BLOCK + slots % BLOCK).astype(jnp.int32)


def draw_image_spans(key, part):
    key = jax.random.fold_in(key, 4)
    stretch = TOKENS // SPANS
    tiles = jax.random.randint(key, (SPANS,), 1, 4).astype(jnp.int32)
    offset = jax.random.randint(jax.random.fold_in(key, 1), (SPANS,), 0, stretch - tiles * IMG_TOK + 1).astype(jnp.int32)
    index = jnp.arange(SPANS, dtype=jnp.int32)
    offset = jnp.where(index == SPANS - 1, stretch - tiles * IMG_TOK, offset)
    offset = jnp.where(index == 0, 0, offset).astype(jnp.int32)
    starts = index * stretch + offset
    return jnp.stack([starts, starts + tiles * IMG_TOK]).astype(jnp.int32)


def level_of(own_key, dims, cuts, low, high):
    loudness, own = 1.0, jax.random.fold_in(own_key, 6)
    for axis_at, parts in cuts:
        steps = jnp.exp(jax.random.uniform(jax.random.fold_in(own, axis_at), (parts,), jnp.float32, low / len(cuts), high / len(cuts)))
        loudness = loudness * jnp.repeat(steps, dims[axis_at] // parts).reshape([-1 if axis == axis_at else 1 for axis in range(len(dims))])
    return loudness


def split_up(amount, total, limit, lean):
    weights = [(1 << 20) // math.isqrt(rank ** lean) + 1 for rank in range(2, amount + 1)]
    surplus, given = total - limit - (amount - 1), [1] * (amount - 1)
    while surplus > 0:
        movable = [i for i in range(amount - 1) if given[i] < limit]
        pool, budget = sum([weights[i] for i in movable]), surplus
        for i in movable:
            addition = min(limit - given[i], max(1, budget * weights[i] // pool), surplus)
            given[i] = given[i] + addition
            surplus = surplus - addition
    return np.array([limit] + given)


def ragged(rng, count, total, reach, slope):
    if count == 2:
        one = jax.random.randint(rng, (), max(1, total - reach), min(reach, total - 1) + 1)
        return jnp.stack([one, total - one])
    sizes = jnp.asarray(split_up(count, total, reach, slope), jnp.int32)
    couples = (count - 1) // 2
    donor, sink = sizes[1:1 + 2 * couples:2], sizes[2:2 + 2 * couples:2]
    margin = jnp.minimum(donor - 1, reach - sink)
    moved = jax.random.randint(jax.random.fold_in(rng, 1), (couples,), 0, 1 << 20) % (margin + 1)
    sizes = sizes.at[1:1 + 2 * couples:2].set(donor - moved).at[2:2 + 2 * couples:2].set(sink + moved)
    return sizes[jax.random.permutation(jax.random.fold_in(rng, 2), count)]


def gaussian(own_key, shape, scale, bound, shards=(), kind=jnp.bfloat16):
    drawn = scale * jax.random.normal(own_key, shape, jnp.float32)
    if shards:
        drawn = drawn * level_of(own_key, shape, shards, -0.22, 0.18)
    return jnp.clip(drawn, -bound, bound).astype(kind)


def setup_inputs(seed: int = 0) -> dict:
    arg_keys = jax.random.split(jax.random.key(seed), 8)
    return {
        "queries": draw_queries(jax.random.fold_in(arg_keys[7], 71), 0),
        "keys": draw_keys(jax.random.fold_in(arg_keys[7], 71), 0),
        "values": gaussian(arg_keys[2], (TOKENS, KVH * DH), 2.0, 8.0, ((0, 16), (1, 8))),
        "positions": draw_positions(jax.random.fold_in(arg_keys[7], 71), 0),
        "doc_lengths": ragged(arg_keys[4], DOCS, TOKENS, TOKENS // 4, 2).astype(jnp.int32),
        "image_spans": draw_image_spans(jax.random.fold_in(arg_keys[7], 71), 0),
        "out_weight": gaussian(arg_keys[6], (HQ * DH, D), (HQ * DH) ** -0.5, 0.0625, ((0, 8), (1, 16))),
    }


NEGATIVE = -1e+30

def token_labels(places, doc_lengths, image_spans):
    doc_ends = jnp.cumsum(doc_lengths)
    document = lax.optimization_barrier(jnp.sum((places[:, None] >= doc_ends[None, :]).astype(jnp.int32), axis=1))
    inside = (places[:, None] >= image_spans[0][None, :]) & (places[:, None] < image_spans[1][None, :])
    numbers = jnp.arange(1, image_spans.shape[1] + 1, dtype=jnp.int32)
    image = lax.optimization_barrier(jnp.sum(jnp.where(inside, numbers[None, :], 0), axis=1)).astype(jnp.int32)
    return (document, image)

def visible(query_place, query_doc, query_img, key_place, key_doc, key_img):
    same_doc = query_doc[:, None] == key_doc[None, :]
    earlier = key_place[None, :] <= query_place[:, None]
    same_img = (query_img[:, None] == key_img[None, :]) & (query_img[:, None] > 0)
    return same_doc & (earlier | same_img)

def reference(queries, keys, values, positions, doc_lengths, image_spans, out_weight):
    document, image = token_labels(positions, doc_lengths, image_spans)
    allowed = visible(positions, document, image, positions, document, image)
    scale = 1.0 / math.sqrt(DH)
    group = HQ // KVH
    query_heads = queries.reshape(TOKENS, HQ, DH).transpose(1, 0, 2)
    key_heads = keys.reshape(TOKENS, KVH, DH).transpose(1, 0, 2)
    value_heads = values.reshape(TOKENS, KVH, DH).transpose(1, 0, 2)

    def one_head(head):
        query_one = query_heads[head]
        key_one = key_heads[head // group]
        value_one = value_heads[head // group]
        scores = jnp.dot(query_one, key_one.T, preferred_element_type=jnp.float32) * scale
        top = lax.optimization_barrier(jnp.max(jnp.where(allowed, scores, NEGATIVE), axis=1, keepdims=True))
        expo = jnp.where(allowed, jnp.exp(scores - top), 0.0)
        total = lax.optimization_barrier(jnp.sum(expo, axis=1, keepdims=True))
        mixed = jnp.dot(expo.astype(jnp.bfloat16), value_one, preferred_element_type=jnp.float32)
        return mixed / total
    attended = lax.map(one_head, jnp.arange(HQ, dtype=jnp.int32)).astype(jnp.bfloat16)
    flat = attended.transpose(1, 0, 2).reshape(TOKENS, HQ * DH)
    return jnp.dot(flat, out_weight, preferred_element_type=jnp.float32).astype(jnp.bfloat16)
```

```python
import functools
import math

import jax
import jax.numpy as jnp
from jax import lax
from jax.experimental import pallas as pl
from jax.experimental.pallas import tpu as pltpu
from jax.sharding import Mesh
from jax.sharding import PartitionSpec as P

DH = 128
RUN = 64
CHUNK = 256
MAX_CHUNKS = 10
NEGATIVE = -1e30
Z = ("zh", "zl")
Z_ORDER = (0, -1, 1, 2)


def z_index():
    return lax.axis_index("zh") * 2 + lax.axis_index("zl")


def shift(value, axis, step):
    return lax.ppermute(value, axis, [(i, (i + step) % 4) for i in range(4)])


def swap_cores(value):
    return lax.ppermute(value, "c", [(0, 1), (1, 0)])


def attend_kernel(pos, lengths, spans, q, kv, left, right, left2, right2, out, ks, vs, ss, top, tot, acc):
    z, x = z_index(), lax.axis_index("x")
    rows, heads = q.shape[0], q.shape[1] // DH
    runs = rows // RUN

    def place(ref, row, group):
        for i in range(runs):
            at = pl.multiple_of(pos[(group * runs + i) * RUN], RUN)
            ks[pl.ds(at, RUN), :] = ref[row + RUN * i : row + RUN * (i + 1), :]
            vs[pl.ds(at, RUN), :] = ref[row + rows + RUN * i : row + rows + RUN * (i + 1), :]

    for ref, step, held in (
        (kv, 0, (0, 1, 2, 3)),
        (left, -1, (0, 1, 2, 3)),
        (right, 1, (0, 1, 2, 3)),
        (left2, 2, (0, 1)),
        (right2, 2, (2, 3)),
    ):
        for n, j in enumerate(held):
            group = lax.rem(z + Z_ORDER[j] + 4, 4) * 4 + lax.rem(x + step + 4, 4)
            place(ref, 2 * rows * n, group)

    ends = []
    for d in range(lengths.shape[0]):
        ends.append(lengths[d] + (ends[-1] if ends else 0))
    starts = [0] + ends[:-1]
    span_list = [(spans[0, k], spans[1, k]) for k in range(spans.shape[1])]

    def interval(at):
        low = jnp.zeros_like(at)
        end = jnp.zeros_like(at)
        for first, last in zip(starts, ends):
            inside = (at >= first) & (at < last)
            low = jnp.where(inside, first, low)
            end = jnp.where(inside, last, end)
        high = at + 1
        for first, last in span_list:
            inside = (at >= first) & (at < last)
            high = jnp.where(inside, jnp.maximum(high, jnp.minimum(last, end)), high)
        return low, high

    scale = math.log2(math.e) / math.sqrt(DH)
    first_group = (z * 4 + x) * runs

    def block(i, _):
        p0 = pos[(first_group + i) * RUN]
        row = pl.multiple_of(i * RUN, RUN)
        at = p0 + lax.broadcasted_iota(jnp.int32, (RUN, DH), 0)
        low, high = interval(at)
        width = high - low
        first_low, _ = interval(p0)
        _, last_high = interval(p0 + RUN - 1)
        first_chunk = first_low // CHUNK
        end_chunk = (last_high + CHUNK - 1) // CHUNK
        lanes = lax.broadcasted_iota(jnp.int32, (RUN, DH), 1) - low
        queries = jnp.concatenate([q[pl.ds(row, RUN), h * DH : (h + 1) * DH] for h in range(heads)], axis=0)
        top[...] = jnp.full_like(top, NEGATIVE)
        tot[...] = jnp.zeros_like(tot)
        acc[...] = jnp.zeros_like(acc)

        def score(j, _):
            start = pl.multiple_of(j * CHUNK, CHUNK)
            keys = ks[pl.ds(start, CHUNK), :]
            s = lax.dot_general(queries, keys, (((1,), (1,)), ((), ())), preferred_element_type=jnp.float32)
            for n in range(CHUNK // DH):
                t = lanes + (start + n * DH)
                allowed = (t >= 0) & (t < width)
                part = s[:, n * DH : (n + 1) * DH].reshape(heads, RUN, DH)
                part = jnp.where(allowed[None], part, NEGATIVE).reshape(heads * RUN, DH)
                ss[j - first_chunk, :, n * DH : (n + 1) * DH] = part
                top[...] = jnp.maximum(top[...], part)
            return 0

        lax.fori_loop(first_chunk, end_chunk, score, 0)
        highest = jnp.max(top[...], axis=1, keepdims=True)

        def mix(j, _):
            start = pl.multiple_of(j * CHUNK, CHUNK)
            expo = jnp.exp2((ss[j - first_chunk] - highest) * scale)
            total = tot[...]
            for n in range(CHUNK // DH):
                total = total + expo[:, n * DH : (n + 1) * DH]
            tot[...] = total
            acc[...] += jnp.dot(expo.astype(jnp.bfloat16), vs[pl.ds(start, CHUNK), :], preferred_element_type=jnp.float32)
            return 0

        lax.fori_loop(first_chunk, end_chunk, mix, 0)
        total = jnp.sum(tot[...], axis=1, keepdims=True)
        mixed = (acc[...] / total).astype(jnp.bfloat16)
        for h in range(heads):
            out[pl.ds(row, RUN), h * DH : (h + 1) * DH] = mixed[h * RUN : (h + 1) * RUN]
        return 0

    lax.fori_loop(0, runs, block, 0)


def attend(positions, lengths, spans, q, pieces):
    rows = q.shape[0]
    stacked = q.shape[1] // DH * RUN
    smem = pl.BlockSpec(memory_space=pltpu.SMEM)
    vmem = pl.BlockSpec(memory_space=pltpu.VMEM)
    slots = positions.shape[0]
    return pl.pallas_call(
        attend_kernel,
        out_shape=jax.ShapeDtypeStruct(q.shape, jnp.bfloat16),
        in_specs=[smem] * 3 + [vmem] * (1 + len(pieces)),
        out_specs=vmem,
        scratch_shapes=[
            pltpu.VMEM((slots, DH), jnp.bfloat16),
            pltpu.VMEM((slots, DH), jnp.bfloat16),
            pltpu.VMEM((MAX_CHUNKS, stacked, CHUNK), jnp.float32),
            pltpu.VMEM((stacked, DH), jnp.float32),
            pltpu.VMEM((stacked, DH), jnp.float32),
            pltpu.VMEM((stacked, DH), jnp.float32),
        ],
        compiler_params=pltpu.CompilerParams(vmem_limit_bytes=40 * 2**20),
        cost_estimate=pl.CostEstimate(
            flops=4 * rows * slots // 4 * q.shape[1], bytes_accessed=4 * 2**20, transcendentals=rows * slots * 2
        ),
        name="attend",
    )(positions, lengths, spans, q, *pieces)


def project_kernel(steps, *refs):
    own, left, right, left2, right2, w0, wl, wr, wl2, wr2 = refs[:10]
    outs = refs[10 : 10 + 2 * len(steps)]
    rows, weights, row_sems, weight_sems = refs[10 + 2 * len(steps) :]
    z, x, y, core = z_index(), lax.axis_index("x"), lax.axis_index("y"), lax.axis_index("c")
    count, half = own.shape[0], own.shape[0] // 2
    depth = w0.shape[0] // 2

    copies = []
    x2 = lax.rem(x + 2, 4)
    for n, (ref, target) in enumerate(
        (
            (own, rows.at[x]),
            (left, rows.at[lax.rem(x + 3, 4)]),
            (right, rows.at[lax.rem(x + 1, 4)]),
            (left2, rows.at[x2, pl.ds(0, half)]),
            (right2, rows.at[x2, pl.ds(half, half)]),
        )
    ):
        copies.append(pltpu.make_async_copy(ref, target, row_sems.at[n]))
    for copy in copies:
        copy.start()

    def weight_copies(n, offset):
        if offset == 2:
            return [
                pltpu.make_async_copy(wl2, weights.at[n, pl.ds(0, depth)], weight_sems.at[n, 0]),
                pltpu.make_async_copy(wr2, weights.at[n, pl.ds(depth, depth)], weight_sems.at[n, 1]),
            ]
        ref = {0: w0, 1: wr, 3: wl}[offset]
        return [pltpu.make_async_copy(ref, weights.at[n], weight_sems.at[n, 0])]

    for n, step in enumerate(steps):
        wanted = lax.rem(y + step + 4 - z + 4, 4)
        for offset in range(4):

            @pl.when(wanted == offset)
            def _():
                for copy in weight_copies(n, offset):
                    copy.start()

    for copy in copies:
        copy.wait()
    for n, step in enumerate(steps):
        wanted = lax.rem(y + step + 4 - z + 4, 4)
        for offset in range(4):

            @pl.when(wanted == offset)
            def _():
                for copy in weight_copies(n, offset):
                    copy.wait()

        for which, first in ((1, 2 - 2 * core), (0, 2 * core)):
            for j in range(2):
                outs[2 * n + which][j * count : (j + 1) * count, :] = jnp.dot(
                    rows[first + j], weights[n], preferred_element_type=jnp.float32
                ).astype(jnp.bfloat16)


def project(steps, att_pieces, w_pieces):
    any_ = pl.BlockSpec(memory_space=pl.ANY)
    vmem = pl.BlockSpec(memory_space=pltpu.VMEM)
    count, depth = att_pieces[0].shape
    width = w_pieces[0].shape[1]
    n = len(steps)
    return pl.pallas_call(
        functools.partial(project_kernel, steps),
        out_shape=[jax.ShapeDtypeStruct((2 * count, width), jnp.bfloat16)] * (2 * n),
        in_specs=[any_] * 10,
        out_specs=[vmem] * (2 * n),
        scratch_shapes=[
            pltpu.VMEM((4, count, depth), jnp.bfloat16),
            pltpu.VMEM((n, depth, width), jnp.bfloat16),
            pltpu.SemaphoreType.DMA((5,)),
            pltpu.SemaphoreType.DMA((n, 2)),
        ],
        compiler_params=pltpu.CompilerParams(vmem_limit_bytes=40 * 2**20),
        cost_estimate=pl.CostEstimate(
            flops=2 * 4 * count * depth * width * n, bytes_accessed=(4 + 2 * n) * 2**20, transcendentals=0
        ),
        name="project",
    )(*att_pieces, *w_pieces)


def plus(*parts):
    total = parts[0].astype(jnp.float32)
    for part in parts[1:]:
        total = total + part.astype(jnp.float32)
    return total.astype(jnp.bfloat16)


def ring_gather(value, axis):
    half = value.shape[0] // 2
    left = shift(value, axis, 1)
    right = shift(value, axis, -1)
    left2 = shift(left[:half], axis, 1)
    right2 = shift(right[half:], axis, -1)
    return value, left, right, left2, right2


def shards(queries, keys, values, positions, lengths, spans, weight):
    count = queries.shape[0]
    kv = jnp.concatenate([keys, values], axis=0)
    line = [kv, shift(kv, Z, 1), shift(kv, Z, -1), shift(kv, Z, 2)]
    line = jnp.concatenate(line, axis=0)
    line, weight = lax.optimization_barrier((line, weight))
    pieces = ring_gather(line, "x")
    w_pieces = ring_gather(weight, Z)
    attended = attend(positions, lengths, spans, queries, pieces)
    att_pieces = ring_gather(attended, "x")

    keep2, send2 = project((2,), att_pieces, w_pieces)
    far = plus(keep2, swap_cores(send2))
    from_left = shift(far[:count], "y", 1)
    from_right = shift(far[count:], "y", -1)
    keep_up, send_up, keep_down, send_down = project((1, -1), att_pieces, w_pieces)
    up = plus(keep_up, swap_cores(send_up))
    down = plus(keep_down, swap_cores(send_down))
    up = jnp.concatenate([plus(up[:count], from_left), up[count:]], axis=0)
    down = jnp.concatenate([down[:count], plus(down[count:], from_right)], axis=0)
    from_below = shift(up, "y", 1)
    from_above = shift(down, "y", -1)
    keep0, send0 = project((0,), att_pieces, w_pieces)
    total = plus(keep0, swap_cores(send0), from_below, from_above)

    low = lax.rem(lax.axis_index("x"), 2)
    same = lax.dynamic_slice_in_dim(total, low * count, count, 0)
    other = lax.dynamic_slice_in_dim(total, (1 - low) * count, count, 0)

    def pairs(flip):
        return [
            ((2 * a + b) * 2 + c, (2 * c + (b ^ flip)) * 2 + a) for a in range(2) for b in range(2) for c in range(2)
        ]

    same = lax.ppermute(same, ("x", "c"), pairs(0))
    other = lax.ppermute(other, ("x", "c"), pairs(1))
    return jnp.where(
        low == 0, jnp.concatenate([same, other], axis=1), jnp.concatenate([other, same], axis=1)
    )


def solution(mesh):
    fine = Mesh(mesh.devices.reshape(2, 2, 4, 4, 2), ("zh", "zl", "x", "y", "c"))
    rows, columns = ("zh", "zl", "x"), ("y", "c")
    return jax.shard_map(
        shards,
        mesh=fine,
        in_specs=(P(rows, columns), P(rows, columns), P(rows, columns), P(), P(), P(), P(columns, rows)),
        out_specs=P(rows, columns),
        check_vma=False,
    )
```

```python
import functools
import math

import jax
import jax.numpy as jnp
from jax import lax
from jax.experimental import pallas as pl
from jax.experimental.pallas import tpu as pltpu
from jax.sharding import Mesh
from jax.sharding import PartitionSpec as P

DH = 128
RUN = 64
SIZES = (256, 512, 768, 1024, 1152, 1536, 2304)
NEGATIVE = -1e30
Z = ("zh", "zl")


def z_index():
    return lax.axis_index("zh") * 2 + lax.axis_index("zl")


def shift(value, axis, step):
    return lax.ppermute(value, axis, [(i, (i + step) % 4) for i in range(4)])


def swap_cores(value):
    return lax.ppermute(value, "c", [(0, 1), (1, 0)])


def plus(first, second):
    return (first.astype(jnp.float32) + second.astype(jnp.float32)).astype(jnp.bfloat16)


SMEM = pl.BlockSpec(memory_space=pltpu.SMEM)
VMEM = pl.BlockSpec(memory_space=pltpu.VMEM)


def place_kernel(held, pos, *refs):
    blocks, outs = refs[: len(held)], refs[-2:]
    z, x = z_index(), lax.axis_index("x")
    for ref, items in zip(blocks, held):
        rows = ref.shape[0] // len(items)
        runs = rows // RUN
        for n, (dz, dx, which) in enumerate(items):
            group = lax.rem(z + dz, 4) * 4 + lax.rem(x + dx, 4)
            for i in range(runs):
                at = pl.multiple_of(pos[group * runs + i], RUN)
                row = n * rows + i * RUN
                outs[which][pl.ds(at, RUN), :] = ref[row : row + RUN, :]


def place(positions, held, blocks, ordered=None):
    shape = jax.ShapeDtypeStruct((positions.shape[0] * RUN, DH), jnp.bfloat16)
    old = list(ordered or ())
    at = 1 + len(blocks)
    return pl.pallas_call(
        functools.partial(place_kernel, held),
        out_shape=[shape, shape],
        in_specs=[SMEM] + [VMEM] * (len(blocks) + len(old)),
        out_specs=[VMEM, VMEM],
        input_output_aliases={at: 0, at + 1: 1} if old else {},
        compiler_params=pltpu.CompilerParams(vmem_limit_bytes=8 * 2**20),
        cost_estimate=pl.CostEstimate(flops=0, bytes_accessed=2 * 2**20, transcendentals=0),
        name="place",
    )(positions, *blocks, *old)


def attend_kernel(first_row, pos, lengths, spans, q, ks, vs, out):
    z, x = z_index(), lax.axis_index("x")
    heads, slots = out.shape[1] // DH, ks.shape[0]
    runs = out.shape[0] // RUN

    ends = []
    for d in range(lengths.shape[0]):
        ends.append(lengths[d] + (ends[-1] if ends else 0))
    starts = [0] + ends[:-1]
    span_list = [(spans[0, k], spans[1, k]) for k in range(spans.shape[1])]

    def interval(at):
        low = jnp.zeros_like(at)
        end = jnp.zeros_like(at)
        for first, last in zip(starts, ends):
            inside = (at >= first) & (at < last)
            low = jnp.where(inside, first, low)
            end = jnp.where(inside, last, end)
        high = at + 1
        for first, last in span_list:
            inside = (at >= first) & (at < last)
            high = jnp.where(inside, jnp.maximum(high, jnp.minimum(last, end)), high)
        return low, high

    scale = math.log2(math.e) / math.sqrt(DH)
    first_run = (z * 4 + x) * (q.shape[0] // RUN) + first_row // RUN

    def block(i, _):
        p0 = pos[first_run + i]
        row = pl.multiple_of(i * RUN, RUN)
        low, high = interval(p0 + lax.broadcasted_iota(jnp.int32, (RUN, DH), 0))
        width = high - low
        lanes = lax.broadcasted_iota(jnp.int32, (RUN, DH), 1) - low
        first_low, _ = interval(p0)
        _, last_high = interval(p0 + RUN - 1)
        base = first_low // RUN * RUN
        need = last_high - base

        def work(size, groups):
            start = pl.multiple_of(jnp.minimum(base, slots - size), RUN)
            allowed = []
            for n in range(size // DH):
                t = lanes + (start + n * DH)
                allowed.append((t >= 0) & (t < width))
            per = heads // groups
            for g in range(groups):
                columns = [(g * per + h) * DH for h in range(per)]
                queries = jnp.concatenate(
                    [q[pl.ds(first_row + row, RUN), c : c + DH] for c in columns], axis=0
                )
                s = lax.dot_general(
                    queries,
                    ks[pl.ds(start, size), :],
                    (((1,), (1,)), ((), ())),
                    preferred_element_type=jnp.float32,
                )
                parts = [
                    jnp.where(
                        allowed[n][None], s[:, n * DH : (n + 1) * DH].reshape(per, RUN, DH), NEGATIVE
                    ).reshape(per * RUN, DH)
                    for n in range(size // DH)
                ]
                top = jnp.max(functools.reduce(jnp.maximum, parts), axis=1, keepdims=True)
                expo = [jnp.exp2((part - top) * scale) for part in parts]
                total = jnp.sum(functools.reduce(jnp.add, expo), axis=1, keepdims=True)
                weights = jnp.concatenate([e.astype(jnp.bfloat16) for e in expo], axis=1)
                mixed = jnp.dot(weights, vs[pl.ds(start, size), :], preferred_element_type=jnp.float32)
                mixed = (mixed / total).astype(jnp.bfloat16)
                for h, c in enumerate(columns):
                    out[pl.ds(row, RUN), c : c + DH] = mixed[h * RUN : (h + 1) * RUN]

        below = 0
        for size in SIZES:

            @pl.when((need > below) & (need <= size))
            def _():
                work(size, 2 if size <= 1152 else 4)

            below = size
        return 0

    lax.fori_loop(0, runs, block, 0)


def attend(first_row, rows, positions, lengths, spans, q, ordered):
    width = q.shape[1]
    return pl.pallas_call(
        functools.partial(attend_kernel, first_row),
        out_shape=jax.ShapeDtypeStruct((rows, width), jnp.bfloat16),
        in_specs=[SMEM] * 3 + [VMEM] * 3,
        out_specs=VMEM,
        compiler_params=pltpu.CompilerParams(vmem_limit_bytes=16 * 2**20),
        cost_estimate=pl.CostEstimate(
            flops=4 * rows * 1024 * width, bytes_accessed=4 * 2**20, transcendentals=rows * 8 * width
        ),
        name="attend",
    )(positions, lengths, spans, q, *ordered)


def join_kernel(ranges, *refs):
    row = 0
    for ref, (first, last) in zip(refs, ranges):
        refs[-1][row : row + last - first, :] = ref[first:last, :]
        row += last - first


def join(pieces, ranges):
    rows = sum(last - first for first, last in ranges)
    return pl.pallas_call(
        functools.partial(join_kernel, ranges),
        out_shape=jax.ShapeDtypeStruct((rows, pieces[0].shape[1]), pieces[0].dtype),
        in_specs=[VMEM] * len(pieces),
        out_specs=VMEM,
        compiler_params=pltpu.CompilerParams(vmem_limit_bytes=4 * 2**20),
        cost_estimate=pl.CostEstimate(flops=0, bytes_accessed=2**20, transcendentals=0),
        name="join",
    )(*pieces)


def project_kernel(core_zero, core_one, *refs):
    pieces = refs[: len(core_zero) + len(core_one)]
    weights = refs[len(pieces) : -3]
    keep, send, rows = refs[-3:]
    core = lax.axis_index("c")
    for mine, names in ((core, core_zero), (1 - core, core_one)):
        at = 0
        for n in names:
            rows[mine, at : at + pieces[n].shape[0], :] = pieces[n][...]
            at += pieces[n].shape[0]
    for target, which in ((send, 1), (keep, 0)):
        for n, parts in enumerate(BLOCKS):
            total, at = None, 0
            for part in parts:
                depth = weights[part].shape[0]
                share = jnp.dot(rows[which, :, at : at + depth], weights[part][...], preferred_element_type=jnp.float32)
                total = share if total is None else total + share
                at += depth
            target[n] = total.astype(jnp.bfloat16)


BLOCKS = ((0,), (1,), (2,), (3, 4))


def project(pieces, core_zero, core_one, weights):
    count, depth = sum(pieces[n].shape[0] for n in core_zero), pieces[0].shape[1]
    width = weights[0].shape[1]
    result = jax.ShapeDtypeStruct((len(BLOCKS), count, width), jnp.bfloat16)
    return pl.pallas_call(
        functools.partial(project_kernel, core_zero, core_one),
        out_shape=[result, result],
        in_specs=[VMEM] * (len(pieces) + len(weights)),
        out_specs=[VMEM, VMEM],
        scratch_shapes=[pltpu.VMEM((2, count, depth), jnp.bfloat16)],
        compiler_params=pltpu.CompilerParams(vmem_limit_bytes=16 * 2**20),
        cost_estimate=pl.CostEstimate(
            flops=4 * count * depth * width * len(BLOCKS), bytes_accessed=4 * 2**20, transcendentals=0
        ),
        name="project",
    )(*pieces, *weights)


def combine_kernel(keep, got, *refs):
    outs, stack = refs[:-1], refs[-1]
    z, y, core = z_index(), lax.axis_index("y"), lax.axis_index("c")
    for block, away in enumerate((0, 3, 1, 2)):
        ahead = lax.rem(away + z - y + 4, 4)
        turn = lax.rem(jnp.where(core == 0, 3 - ahead, ahead + 3), 4)
        stack[turn] = plus(keep[block], got[block])
    for n, out in enumerate(outs):
        out[...] = stack[n]


def combine(keep, got):
    _, rows, width = keep.shape
    result = jax.ShapeDtypeStruct((rows, width), jnp.bfloat16)
    return pl.pallas_call(
        combine_kernel,
        out_shape=[result] * 4,
        in_specs=[VMEM] * 2,
        out_specs=[VMEM] * 4,
        scratch_shapes=[pltpu.VMEM(keep.shape, jnp.bfloat16)],
        compiler_params=pltpu.CompilerParams(vmem_limit_bytes=8 * 2**20),
        cost_estimate=pl.CostEstimate(flops=0, bytes_accessed=3 * 2**20, transcendentals=0),
        name="combine",
    )(keep, got)


def relay(value, axis):
    pairs = [(2 * i + c, 2 * ((i + 1 - 2 * c) % 4) + c) for i in range(4) for c in range(2)]
    return lax.ppermute(value, (axis, "c"), pairs)


def home(value, away, turn):
    pairs = []
    for x in range(4):
        for y in range(4):
            for c in range(2):
                to_y = (y + (1 - 2 * c) * turn) % 4
                pairs.append(((x * 4 + y) * 2 + c, (((x + away[c]) % 4) * 4 + to_y) * 2 + x // 2))
    return lax.ppermute(value, ("x", "y", "c"), pairs)


def sum_shares(turns, away):
    stay = home(turns[3], away, 0)
    passed = relay(turns[0], "y")
    passed = relay(plus(turns[1], passed), "y")
    return stay, home(plus(turns[2], passed), away, 1)


def after(value, *others):
    return lax.optimization_barrier((value, *others))[0]


def shards(queries, keys, values, positions, lengths, spans, weight):
    x = lax.axis_index("x")
    count = keys.shape[0]
    kv = jnp.concatenate([keys, values], axis=0)
    line = [shift(kv, Z, 1), shift(kv, Z, -1), shift(kv, Z, 2)]
    left, right = shift(kv, "x", 1), shift(kv, "x", -1)
    line = jnp.concatenate(line, axis=0)
    line, weight, left, right = lax.optimization_barrier((line, weight, left, right))
    line_left, line_right = shift(line, "x", 1), shift(line, "x", -1)
    weight_left, weight_right = shift(weight, Z, 1), shift(weight, Z, -1)

    runs = positions.reshape(-1, RUN)[:, 0]
    line_blocks = [(dz, which) for dz in (3, 1, 2) for which in (0, 1)]

    def at_x(dx, blocks=line_blocks):
        return [(dz, dx, which) for dz, which in blocks]

    own = [(0, 0), (0, 1)]
    ordered = place(runs, (at_x(0, own), at_x(0), at_x(3, own), at_x(1, own)), (kv, line, left, right))
    left2 = shift(join((line_left, left), ((0, 3 * count), (0, count))), "x", 1)
    right2 = shift(join((line_right, right), ((3 * count, 6 * count), (count, 2 * count))), "x", -1)
    ordered = place(runs, (at_x(3), at_x(1)), (line_left, line_right), ordered)
    ordered = place(
        runs,
        (at_x(2, line_blocks[:3] + own[:1]), at_x(2, line_blocks[3:] + own[1:])),
        (left2, right2),
        ordered,
    )

    half = count // 2
    upper = attend(0, half, runs, lengths, spans, queries, ordered)
    lower = attend(half, half, runs, lengths, spans, after(queries, upper), ordered)
    upper_left, upper_right = shift(upper, "x", 1), shift(upper, "x", -1)
    lower_left, lower_right = shift(lower, "x", 1), shift(lower, "x", -1)

    middle = weight.shape[0] // 2
    weight_left_far = shift(join((after(weight_left, lower),), ((0, middle),)), Z, 1)
    weight_right_far = shift(join((after(weight_right, lower),), ((middle, 2 * middle),)), Z, -1)
    upper_far, lower_far = shift(upper_left, "x", 1), shift(lower_right, "x", -1)

    weights = (weight, weight_left, weight_right, weight_left_far, weight_right_far)
    rows = (upper_left, lower_left, upper_right, lower_right)
    keep, send = project(rows, (0, 1), (2, 3), weights)
    near = combine(keep, swap_cores(send))
    rows = (upper, lower, after(upper_far, near[0]), lower_far)
    keep, send = project(rows, (0, 1), (2, 3), weights)
    mixed = combine(keep, swap_cores(send))

    near = plus(*sum_shares(near, (-1, 1)))
    mixed = plus(*sum_shares(mixed, (0, 2)))
    return jnp.where(
        lax.rem(x, 2) == 0,
        jnp.concatenate([mixed, near], axis=1),
        jnp.concatenate([near, mixed], axis=1),
    )


def solution(mesh):
    fine = Mesh(mesh.devices.reshape(2, 2, 4, 4, 2), ("zh", "zl", "x", "y", "c"))
    rows, columns = ("zh", "zl", "x"), ("y", "c")
    return jax.shard_map(
        shards,
        mesh=fine,
        in_specs=(P(rows, columns), P(rows, columns), P(rows, columns), P(), P(), P(), P(columns, rows)),
        out_specs=P(rows, columns),
        check_vma=False,
    )
```

```python
import functools
import math

import jax
import jax.numpy as jnp
from jax import lax
from jax.experimental import pallas as pl
from jax.experimental.pallas import tpu as pltpu
from jax.sharding import Mesh
from jax.sharding import PartitionSpec as P

DH = 128
RUN = 64
SIZES = (256, 512, 768, 1024, 1152, 1536, 2304)
NEGATIVE = -1e30
Z = ("zh", "zl")


def z_index():
    return lax.axis_index("zh") * 2 + lax.axis_index("zl")


def shift(value, axis, step):
    return lax.ppermute(value, axis, [(i, (i + step) % 4) for i in range(4)])


def swap_cores(value):
    return lax.ppermute(value, "c", [(0, 1), (1, 0)])


def plus(first, second):
    return (first.astype(jnp.float32) + second.astype(jnp.float32)).astype(jnp.bfloat16)


SMEM = pl.BlockSpec(memory_space=pltpu.SMEM)
VMEM = pl.BlockSpec(memory_space=pltpu.VMEM)


def place_kernel(held, pos, *refs):
    blocks, outs = refs[: len(held)], refs[-2:]
    z, x = z_index(), lax.axis_index("x")
    for ref, items in zip(blocks, held):
        rows = ref.shape[0] // len(items)
        runs = rows // RUN
        for n, (dz, dx, which) in enumerate(items):
            group = lax.rem(z + dz, 4) * 4 + lax.rem(x + dx, 4)
            for i in range(runs):
                at = pl.multiple_of(pos[group * runs + i], RUN)
                row = n * rows + i * RUN
                outs[which][pl.ds(at, RUN), :] = ref[row : row + RUN, :]


def place(positions, held, blocks, ordered=None):
    shape = jax.ShapeDtypeStruct((positions.shape[0] * RUN, DH), jnp.bfloat16)
    old = list(ordered or ())
    at = 1 + len(blocks)
    return pl.pallas_call(
        functools.partial(place_kernel, held),
        out_shape=[shape, shape],
        in_specs=[SMEM] + [VMEM] * (len(blocks) + len(old)),
        out_specs=[VMEM, VMEM],
        input_output_aliases={at: 0, at + 1: 1} if old else {},
        compiler_params=pltpu.CompilerParams(vmem_limit_bytes=8 * 2**20),
        cost_estimate=pl.CostEstimate(flops=0, bytes_accessed=2 * 2**20, transcendentals=0),
        name="place",
    )(positions, *blocks, *old)


def attend_kernel(first_row, pos, lengths, spans, q, ks, vs, out):
    z, x = z_index(), lax.axis_index("x")
    heads, slots = out.shape[1] // DH, ks.shape[0]
    runs = out.shape[0] // RUN

    ends = []
    for d in range(lengths.shape[0]):
        ends.append(lengths[d] + (ends[-1] if ends else 0))
    starts = [0] + ends[:-1]
    span_list = [(spans[0, k], spans[1, k]) for k in range(spans.shape[1])]

    def interval(at):
        low = jnp.zeros_like(at)
        end = jnp.zeros_like(at)
        for first, last in zip(starts, ends):
            inside = (at >= first) & (at < last)
            low = jnp.where(inside, first, low)
            end = jnp.where(inside, last, end)
        high = at + 1
        for first, last in span_list:
            inside = (at >= first) & (at < last)
            high = jnp.where(inside, jnp.maximum(high, jnp.minimum(last, end)), high)
        return low, high

    scale = math.log2(math.e) / math.sqrt(DH)
    first_run = (z * 4 + x) * (q.shape[0] // RUN) + first_row // RUN

    def block(i, _):
        p0 = pos[first_run + i]
        row = pl.multiple_of(i * RUN, RUN)
        low, high = interval(p0 + lax.broadcasted_iota(jnp.int32, (RUN, DH), 0))
        width = high - low
        lanes = lax.broadcasted_iota(jnp.int32, (RUN, DH), 1) - low
        first_low, _ = interval(p0)
        _, last_high = interval(p0 + RUN - 1)
        base = first_low // RUN * RUN
        need = last_high - base

        def work(size, groups):
            start = pl.multiple_of(jnp.minimum(base, slots - size), RUN)
            allowed = []
            for n in range(size // DH):
                t = lanes + (start + n * DH)
                allowed.append((t >= 0) & (t < width))
            per = heads // groups
            for g in range(groups):
                columns = [(g * per + h) * DH for h in range(per)]
                queries = jnp.concatenate(
                    [q[pl.ds(first_row + row, RUN), c : c + DH] for c in columns], axis=0
                )
                s = lax.dot_general(
                    queries,
                    ks[pl.ds(start, size), :],
                    (((1,), (1,)), ((), ())),
                    preferred_element_type=jnp.float32,
                )
                parts = [
                    jnp.where(
                        allowed[n][None], s[:, n * DH : (n + 1) * DH].reshape(per, RUN, DH), NEGATIVE
                    ).reshape(per * RUN, DH)
                    for n in range(size // DH)
                ]
                top = jnp.max(functools.reduce(jnp.maximum, parts), axis=1, keepdims=True)
                expo = [jnp.exp2((part - top) * scale) for part in parts]
                total = jnp.sum(functools.reduce(jnp.add, expo), axis=1, keepdims=True)
                weights = jnp.concatenate([e.astype(jnp.bfloat16) for e in expo], axis=1)
                mixed = jnp.dot(weights, vs[pl.ds(start, size), :], preferred_element_type=jnp.float32)
                mixed = (mixed / total).astype(jnp.bfloat16)
                for h, c in enumerate(columns):
                    out[pl.ds(row, RUN), c : c + DH] = mixed[h * RUN : (h + 1) * RUN]

        below = 0
        for size in SIZES:

            @pl.when((need > below) & (need <= size))
            def _():
                work(size, 2 if size <= 1152 else 4)

            below = size
        return 0

    lax.fori_loop(0, runs, block, 0)


def attend(first_row, rows, positions, lengths, spans, q, ordered):
    width = q.shape[1]
    return pl.pallas_call(
        functools.partial(attend_kernel, first_row),
        out_shape=jax.ShapeDtypeStruct((rows, width), jnp.bfloat16),
        in_specs=[SMEM] * 3 + [VMEM] * 3,
        out_specs=VMEM,
        compiler_params=pltpu.CompilerParams(vmem_limit_bytes=16 * 2**20),
        cost_estimate=pl.CostEstimate(
            flops=24 * rows * 1024 * width, bytes_accessed=4 * 2**20, transcendentals=rows * 8 * width
        ),
        name="attend",
    )(positions, lengths, spans, q, *ordered)


def join_kernel(ranges, *refs):
    row = 0
    for ref, (first, last) in zip(refs, ranges):
        refs[-1][row : row + last - first, :] = ref[first:last, :]
        row += last - first


def join(pieces, ranges):
    rows = sum(last - first for first, last in ranges)
    return pl.pallas_call(
        functools.partial(join_kernel, ranges),
        out_shape=jax.ShapeDtypeStruct((rows, pieces[0].shape[1]), pieces[0].dtype),
        in_specs=[VMEM] * len(pieces),
        out_specs=VMEM,
        compiler_params=pltpu.CompilerParams(vmem_limit_bytes=4 * 2**20),
        cost_estimate=pl.CostEstimate(flops=0, bytes_accessed=2**20, transcendentals=0),
        name="join",
    )(*pieces)


def project_kernel(core_zero, core_one, *refs):
    pieces = refs[: len(core_zero) + len(core_one)]
    weights = refs[len(pieces) : -3]
    keep, send, rows = refs[-3:]
    core = lax.axis_index("c")
    for mine, names in ((core, core_zero), (1 - core, core_one)):
        at = 0
        for n in names:
            rows[mine, at : at + pieces[n].shape[0], :] = pieces[n][...]
            at += pieces[n].shape[0]
    for target, which in ((send, 1), (keep, 0)):
        for n, parts in enumerate(BLOCKS):
            total, at = None, 0
            for part in parts:
                depth = weights[part].shape[0]
                share = jnp.dot(rows[which, :, at : at + depth], weights[part][...], preferred_element_type=jnp.float32)
                total = share if total is None else total + share
                at += depth
            target[n] = total.astype(jnp.bfloat16)


BLOCKS = ((0,), (1,), (2,), (3, 4))


def project(pieces, core_zero, core_one, weights):
    count, depth = sum(pieces[n].shape[0] for n in core_zero), pieces[0].shape[1]
    width = weights[0].shape[1]
    result = jax.ShapeDtypeStruct((len(BLOCKS), count, width), jnp.bfloat16)
    return pl.pallas_call(
        functools.partial(project_kernel, core_zero, core_one),
        out_shape=[result, result],
        in_specs=[VMEM] * (len(pieces) + len(weights)),
        out_specs=[VMEM, VMEM],
        scratch_shapes=[pltpu.VMEM((2, count, depth), jnp.bfloat16)],
        compiler_params=pltpu.CompilerParams(vmem_limit_bytes=16 * 2**20),
        cost_estimate=pl.CostEstimate(
            flops=4 * count * depth * width * len(BLOCKS), bytes_accessed=4 * 2**20, transcendentals=0
        ),
        name="project",
    )(*pieces, *weights)


def combine_kernel(keep, got, *refs):
    outs, stack = refs[:-1], refs[-1]
    z, y, core = z_index(), lax.axis_index("y"), lax.axis_index("c")
    for block, away in enumerate((0, 3, 1, 2)):
        ahead = lax.rem(away + z - y + 4, 4)
        turn = lax.rem(jnp.where(core == 0, 3 - ahead, ahead + 3), 4)
        stack[turn] = plus(keep[block], got[block])
    for n, out in enumerate(outs):
        out[...] = stack[n]


def combine(keep, got):
    _, rows, width = keep.shape
    result = jax.ShapeDtypeStruct((rows, width), jnp.bfloat16)
    return pl.pallas_call(
        combine_kernel,
        out_shape=[result] * 4,
        in_specs=[VMEM] * 2,
        out_specs=[VMEM] * 4,
        scratch_shapes=[pltpu.VMEM(keep.shape, jnp.bfloat16)],
        compiler_params=pltpu.CompilerParams(vmem_limit_bytes=8 * 2**20),
        cost_estimate=pl.CostEstimate(flops=0, bytes_accessed=3 * 2**20, transcendentals=0),
        name="combine",
    )(keep, got)


def relay(value, axis):
    pairs = [(2 * i + c, 2 * ((i + 1 - 2 * c) % 4) + c) for i in range(4) for c in range(2)]
    return lax.ppermute(value, (axis, "c"), pairs)


def home(value, away, turn):
    pairs = []
    for x in range(4):
        for y in range(4):
            for c in range(2):
                to_y = (y + (1 - 2 * c) * turn) % 4
                pairs.append(((x * 4 + y) * 2 + c, (((x + away[c]) % 4) * 4 + to_y) * 2 + x // 2))
    return lax.ppermute(value, ("x", "y", "c"), pairs)


def sum_shares(turns, away):
    stay = home(turns[3], away, 0)
    passed = relay(turns[0], "y")
    passed = relay(plus(turns[1], passed), "y")
    return stay, home(plus(turns[2], passed), away, 1)


def after(value, *others):
    return lax.optimization_barrier((value, *others))[0]


def shards(queries, keys, values, positions, lengths, spans, weight):
    x = lax.axis_index("x")
    count = keys.shape[0]
    kv = jnp.concatenate([keys, values], axis=0)
    line = [shift(kv, Z, 1), shift(kv, Z, -1), shift(kv, Z, 2)]
    left, right = shift(kv, "x", 1), shift(kv, "x", -1)
    line = jnp.concatenate(line, axis=0)
    line, weight, left, right = lax.optimization_barrier((line, weight, left, right))
    line_left, line_right = shift(line, "x", 1), shift(line, "x", -1)
    weight_left, weight_right = shift(weight, Z, 1), shift(weight, Z, -1)

    runs = positions.reshape(-1, RUN)[:, 0]
    line_blocks = [(dz, which) for dz in (3, 1, 2) for which in (0, 1)]

    def at_x(dx, blocks=line_blocks):
        return [(dz, dx, which) for dz, which in blocks]

    own = [(0, 0), (0, 1)]
    ordered = place(runs, (at_x(0, own), at_x(0), at_x(3, own), at_x(1, own)), (kv, line, left, right))
    left2 = shift(join((line_left, left), ((0, 3 * count), (0, count))), "x", 1)
    right2 = shift(join((line_right, right), ((3 * count, 6 * count), (count, 2 * count))), "x", -1)
    ordered = place(runs, (at_x(3), at_x(1)), (line_left, line_right), ordered)
    ordered = place(
        runs,
        (at_x(2, line_blocks[:3] + own[:1]), at_x(2, line_blocks[3:] + own[1:])),
        (left2, right2),
        ordered,
    )

    half = count // 2
    upper = attend(0, half, runs, lengths, spans, queries, ordered)
    lower = attend(half, half, runs, lengths, spans, after(queries, upper), ordered)
    upper_left, upper_right = shift(upper, "x", 1), shift(upper, "x", -1)
    lower_left, lower_right = shift(lower, "x", 1), shift(lower, "x", -1)

    middle = weight.shape[0] // 2
    weight_left_far = shift(join((after(weight_left, lower),), ((0, middle),)), Z, 1)
    weight_right_far = shift(join((after(weight_right, lower),), ((middle, 2 * middle),)), Z, -1)
    upper_far, lower_far = shift(upper_left, "x", 1), shift(lower_right, "x", -1)

    weights = (weight, weight_left, weight_right, weight_left_far, weight_right_far)
    rows = (upper_left, lower_left, upper_right, lower_right)
    keep, send = project(rows, (0, 1), (2, 3), weights)
    near = combine(keep, swap_cores(send))
    rows = (upper, lower, upper_far, lower_far)
    keep, send = project(rows, (0, 1), (2, 3), weights)
    mixed = combine(keep, swap_cores(send))

    near = plus(*sum_shares(near, (-1, 1)))
    mixed = plus(*sum_shares(mixed, (0, 2)))
    return jnp.where(
        lax.rem(x, 2) == 0,
        jnp.concatenate([mixed, near], axis=1),
        jnp.concatenate([near, mixed], axis=1),
    )


def solution(mesh):
    fine = Mesh(mesh.devices.reshape(2, 2, 4, 4, 2), ("zh", "zl", "x", "y", "c"))
    rows, columns = ("zh", "zl", "x"), ("y", "c")
    return jax.shard_map(
        shards,
        mesh=fine,
        in_specs=(P(rows, columns), P(rows, columns), P(rows, columns), P(), P(), P(), P(columns, rows)),
        out_specs=P(rows, columns),
        check_vma=False,
    )
```

```python
import functools
import math

import jax
import jax.numpy as jnp
from jax import lax
from jax.experimental import pallas as pl
from jax.experimental.pallas import tpu as pltpu
from jax.sharding import Mesh
from jax.sharding import PartitionSpec as P

DH = 128
RUN = 64
SIZES = (256, 512, 768, 1024, 1152, 1536, 2304)
NEGATIVE = -1e30
Z = ("zh", "zl")


def z_index():
    return lax.axis_index("zh") * 2 + lax.axis_index("zl")


def shift(value, axis, step):
    return lax.ppermute(value, axis, [(i, (i + step) % 4) for i in range(4)])


def swap_cores(value):
    return lax.ppermute(value, "c", [(0, 1), (1, 0)])


def plus(first, second):
    return (first.astype(jnp.float32) + second.astype(jnp.float32)).astype(jnp.bfloat16)


SMEM = pl.BlockSpec(memory_space=pltpu.SMEM)
VMEM = pl.BlockSpec(memory_space=pltpu.VMEM)


def place_kernel(held, pos, *refs):
    blocks, outs = refs[: len(held)], refs[-2:]
    z, x = z_index(), lax.axis_index("x")
    for ref, items in zip(blocks, held):
        rows = ref.shape[0] // len(items)
        runs = rows // RUN
        for n, (dz, dx, which) in enumerate(items):
            group = lax.rem(z + dz, 4) * 4 + lax.rem(x + dx, 4)
            for i in range(runs):
                at = pl.multiple_of(pos[group * runs + i], RUN)
                row = n * rows + i * RUN
                outs[which][pl.ds(at, RUN), :] = ref[row : row + RUN, :]


def place(positions, held, blocks, ordered=None):
    shape = jax.ShapeDtypeStruct((positions.shape[0] * RUN, DH), jnp.bfloat16)
    old = list(ordered or ())
    at = 1 + len(blocks)
    return pl.pallas_call(
        functools.partial(place_kernel, held),
        out_shape=[shape, shape],
        in_specs=[SMEM] + [VMEM] * (len(blocks) + len(old)),
        out_specs=[VMEM, VMEM],
        input_output_aliases={at: 0, at + 1: 1} if old else {},
        compiler_params=pltpu.CompilerParams(vmem_limit_bytes=8 * 2**20),
        cost_estimate=pl.CostEstimate(flops=0, bytes_accessed=2 * 2**20, transcendentals=0),
        name="place",
    )(positions, *blocks, *old)


def attend_kernel(pos, lengths, spans, q, ks, vs, out):
    z, x = z_index(), lax.axis_index("x")
    heads, slots = out.shape[1] // DH, ks.shape[0]
    runs = out.shape[0] // RUN

    ends = []
    for d in range(lengths.shape[0]):
        ends.append(lengths[d] + (ends[-1] if ends else 0))
    starts = [0] + ends[:-1]
    span_list = [(spans[0, k], spans[1, k]) for k in range(spans.shape[1])]

    def interval(at):
        low = jnp.zeros_like(at)
        end = jnp.zeros_like(at)
        for first, last in zip(starts, ends):
            inside = (at >= first) & (at < last)
            low = jnp.where(inside, first, low)
            end = jnp.where(inside, last, end)
        high = at + 1
        for first, last in span_list:
            inside = (at >= first) & (at < last)
            high = jnp.where(inside, jnp.maximum(high, jnp.minimum(last, end)), high)
        return low, high

    scale = math.log2(math.e) / math.sqrt(DH)
    first_run = (z * 4 + x) * runs

    def block(i, _):
        p0 = pos[first_run + i]
        row = pl.multiple_of(i * RUN, RUN)
        low, high = interval(p0 + lax.broadcasted_iota(jnp.int32, (RUN, DH), 0))
        width = high - low
        lanes = lax.broadcasted_iota(jnp.int32, (RUN, DH), 1) - low
        first_low, _ = interval(p0)
        _, last_high = interval(p0 + RUN - 1)
        base = first_low // RUN * RUN
        need = last_high - base

        def work(size, groups):
            start = pl.multiple_of(jnp.minimum(base, slots - size), RUN)
            allowed = []
            for n in range(size // DH):
                t = lanes + (start + n * DH)
                allowed.append((t >= 0) & (t < width))
            per = heads // groups
            for g in range(groups):
                columns = [(g * per + h) * DH for h in range(per)]
                queries = jnp.concatenate(
                    [q[pl.ds(row, RUN), c : c + DH] for c in columns], axis=0
                )
                s = lax.dot_general(
                    queries,
                    ks[pl.ds(start, size), :],
                    (((1,), (1,)), ((), ())),
                    preferred_element_type=jnp.float32,
                )
                parts = [
                    jnp.where(
                        allowed[n][None], s[:, n * DH : (n + 1) * DH].reshape(per, RUN, DH), NEGATIVE
                    ).reshape(per * RUN, DH)
                    for n in range(size // DH)
                ]
                top = jnp.max(functools.reduce(jnp.maximum, parts), axis=1, keepdims=True)
                expo = [jnp.exp2((part - top) * scale) for part in parts]
                total = jnp.sum(functools.reduce(jnp.add, expo), axis=1, keepdims=True)
                weights = jnp.concatenate([e.astype(jnp.bfloat16) for e in expo], axis=1)
                mixed = jnp.dot(weights, vs[pl.ds(start, size), :], preferred_element_type=jnp.float32)
                mixed = (mixed / total).astype(jnp.bfloat16)
                for h, c in enumerate(columns):
                    out[pl.ds(row, RUN), c : c + DH] = mixed[h * RUN : (h + 1) * RUN]

        below = 0
        for size in SIZES:

            @pl.when((need > below) & (need <= size))
            def _():
                work(size, 2 if size <= 1152 else 4)

            below = size
        return 0

    lax.fori_loop(0, runs, block, 0)


def attend(positions, lengths, spans, q, ordered):
    rows, width = q.shape
    return pl.pallas_call(
        attend_kernel,
        out_shape=jax.ShapeDtypeStruct((rows, width), jnp.bfloat16),
        in_specs=[SMEM] * 3 + [VMEM] * 3,
        out_specs=VMEM,
        compiler_params=pltpu.CompilerParams(vmem_limit_bytes=16 * 2**20),
        cost_estimate=pl.CostEstimate(
            flops=24 * rows * 1024 * width, bytes_accessed=4 * 2**20, transcendentals=rows * 8 * width
        ),
        name="attend",
    )(positions, lengths, spans, q, *ordered)


def join_kernel(ranges, *refs):
    row = 0
    for ref, (first, last) in zip(refs, ranges):
        refs[-1][row : row + last - first, :] = ref[first:last, :]
        row += last - first


def join(pieces, ranges):
    rows = sum(last - first for first, last in ranges)
    return pl.pallas_call(
        functools.partial(join_kernel, ranges),
        out_shape=jax.ShapeDtypeStruct((rows, pieces[0].shape[1]), pieces[0].dtype),
        in_specs=[VMEM] * len(pieces),
        out_specs=VMEM,
        compiler_params=pltpu.CompilerParams(vmem_limit_bytes=4 * 2**20),
        cost_estimate=pl.CostEstimate(flops=0, bytes_accessed=2**20, transcendentals=0),
        name="join",
    )(*pieces)


BLOCKS = ((0,), (1,), (2,), (3, 4))


def product(rows, weights, parts):
    total, at = None, 0
    for part in parts:
        depth = weights[part].shape[0]
        share = jnp.dot(rows[:, at : at + depth], weights[part][...], preferred_element_type=jnp.float32)
        total = share if total is None else total + share
        at += depth
    return total.astype(jnp.bfloat16)


def near_kernel(left, right, *refs):
    weights, (keep, send, rows) = refs[:-3], refs[-3:]
    core = lax.axis_index("c")
    for at in range(0, left.shape[0], 2 * RUN):
        rows[core, at : at + 2 * RUN, :] = left[at : at + 2 * RUN, :]
        rows[1 - core, at : at + 2 * RUN, :] = right[at : at + 2 * RUN, :]
    for target, which in ((send, 1), (keep, 0)):
        for n, parts in enumerate(BLOCKS):
            target[n] = product(rows.at[which], weights, parts)


def own_kernel(rows, *refs):
    weights, out = refs[:-1], refs[-1]
    for n, parts in enumerate(BLOCKS):
        out[n] = product(rows, weights, parts)


def far_kernel(upper, lower, own, *refs):
    weights, (keep, send, rows) = refs[:-3], refs[-3:]
    core = lax.axis_index("c")
    half = upper.shape[0]
    rows[:half, :] = upper[...]
    rows[half:, :] = lower[...]

    def fill(target, other):
        other[...] = own[...]
        for n, parts in enumerate(BLOCKS):
            target[n] = product(rows, weights, parts)

    @pl.when(core == 0)
    def _():
        fill(send, keep)

    @pl.when(core == 1)
    def _():
        fill(keep, send)


def project(kernel, pieces, weights):
    depth, width = weights[0].shape
    count = 2 * pieces[0].shape[0] if kernel is far_kernel else pieces[0].shape[0]
    result = jax.ShapeDtypeStruct((len(BLOCKS), count, width), jnp.bfloat16)
    results = 1 if kernel is own_kernel else 2
    scratch = {
        own_kernel: [],
        near_kernel: [pltpu.VMEM((2, count, depth), jnp.bfloat16)],
        far_kernel: [pltpu.VMEM((count, depth), jnp.bfloat16)],
    }
    return pl.pallas_call(
        kernel,
        out_shape=[result] * results,
        in_specs=[VMEM] * (len(pieces) + len(weights)),
        out_specs=[VMEM] * results,
        scratch_shapes=scratch[kernel],
        compiler_params=pltpu.CompilerParams(vmem_limit_bytes=16 * 2**20),
        cost_estimate=pl.CostEstimate(
            flops=4 * count * depth * width * len(BLOCKS), bytes_accessed=4 * 2**20, transcendentals=0
        ),
        name="project",
    )(*pieces, *weights)


def combine_kernel(keep, got, *refs):
    outs, stack = refs[:-1], refs[-1]
    z, y, core = z_index(), lax.axis_index("y"), lax.axis_index("c")
    for block, away in enumerate((0, 3, 1, 2)):
        ahead = lax.rem(away + z - y + 4, 4)
        turn = lax.rem(jnp.where(core == 0, 3 - ahead, ahead + 3), 4)
        stack[turn] = plus(keep[block], got[block])
    for n, out in enumerate(outs):
        out[...] = stack[n]


def combine(keep, got):
    _, rows, width = keep.shape
    result = jax.ShapeDtypeStruct((rows, width), jnp.bfloat16)
    return pl.pallas_call(
        combine_kernel,
        out_shape=[result] * 4,
        in_specs=[VMEM] * 2,
        out_specs=[VMEM] * 4,
        scratch_shapes=[pltpu.VMEM(keep.shape, jnp.bfloat16)],
        compiler_params=pltpu.CompilerParams(vmem_limit_bytes=8 * 2**20),
        cost_estimate=pl.CostEstimate(flops=0, bytes_accessed=3 * 2**20, transcendentals=0),
        name="combine",
    )(keep, got)


def relay(value, axis):
    pairs = [(2 * i + c, 2 * ((i + 1 - 2 * c) % 4) + c) for i in range(4) for c in range(2)]
    return lax.ppermute(value, (axis, "c"), pairs)


def home(value, away, turn):
    pairs = []
    for x in range(4):
        for y in range(4):
            for c in range(2):
                to_y = (y + (1 - 2 * c) * turn) % 4
                pairs.append(((x * 4 + y) * 2 + c, (((x + away[c]) % 4) * 4 + to_y) * 2 + x // 2))
    return lax.ppermute(value, ("x", "y", "c"), pairs)


def sum_shares(turns, away):
    stay = home(turns[3], away, 0)
    passed = relay(turns[0], "y")
    passed = relay(plus(turns[1], passed), "y")
    return stay, home(plus(turns[2], passed), away, 1)


def after(value, *others):
    return lax.optimization_barrier((value, *others))[0]


def halves(left, right, axis):
    half = left.shape[0] // 2
    return (
        shift(join((left,), ((0, half),)), axis, 1),
        shift(join((right,), ((half, 2 * half),)), axis, -1),
    )


def shards(queries, keys, values, positions, lengths, spans, weight):
    x = lax.axis_index("x")
    count = keys.shape[0]
    kv = jnp.concatenate([keys, values], axis=0)
    line = [shift(kv, Z, 1), shift(kv, Z, -1), shift(kv, Z, 2)]
    left, right = shift(kv, "x", 1), shift(kv, "x", -1)
    line = jnp.concatenate(line, axis=0)
    line, weight, left, right = lax.optimization_barrier((line, weight, left, right))
    line_left, line_right = shift(line, "x", 1), shift(line, "x", -1)
    weight_left, weight_right = shift(weight, Z, 1), shift(weight, Z, -1)

    runs = positions.reshape(-1, RUN)[:, 0]
    line_blocks = [(dz, which) for dz in (3, 1, 2) for which in (0, 1)]

    def at_x(dx, blocks=line_blocks):
        return [(dz, dx, which) for dz, which in blocks]

    here = [(0, 0), (0, 1)]
    ordered = place(runs, (at_x(0, here), at_x(0), at_x(3, here), at_x(1, here)), (kv, line, left, right))
    left2 = shift(join((line_left, left), ((0, 3 * count), (0, count))), "x", 1)
    right2 = shift(join((line_right, right), ((3 * count, 6 * count), (count, 2 * count))), "x", -1)
    ordered = place(runs, (at_x(3), at_x(1)), (line_left, line_right), ordered)
    ordered = place(
        runs,
        (at_x(2, line_blocks[:3] + here[:1]), at_x(2, line_blocks[3:] + here[1:])),
        (left2, right2),
        ordered,
    )

    own = attend(runs, lengths, spans, queries, ordered)
    rows_left, rows_right = shift(own, "x", 1), shift(own, "x", -1)
    rows_far = halves(rows_left, rows_right, "x")
    weight_far = halves(after(weight_left, own), after(weight_right, own), Z)

    weights = (weight, weight_left, weight_right, *weight_far)
    (own,) = project(own_kernel, (own,), weights)
    rows = (after(rows_left, own), rows_right)
    keep, send = project(near_kernel, rows, weights)
    near = combine(keep, swap_cores(send))
    keep, send = project(far_kernel, (*rows_far, own), weights)
    mixed = combine(keep, swap_cores(send))

    near = plus(*sum_shares(near, (-1, 1)))
    mixed = plus(*sum_shares(mixed, (0, 2)))
    return jnp.where(
        lax.rem(x, 2) == 0,
        jnp.concatenate([mixed, near], axis=1),
        jnp.concatenate([near, mixed], axis=1),
    )


def solution(mesh):
    fine = Mesh(mesh.devices.reshape(2, 2, 4, 4, 2), ("zh", "zl", "x", "y", "c"))
    rows, columns = ("zh", "zl", "x"), ("y", "c")
    return jax.shard_map(
        shards,
        mesh=fine,
        in_specs=(P(rows, columns), P(rows, columns), P(rows, columns), P(), P(), P(), P(columns, rows)),
        out_specs=P(rows, columns),
        check_vma=False,
    )
```

```python
import functools
import math

import jax
import jax.numpy as jnp
from jax import lax
from jax.experimental import pallas as pl
from jax.experimental.pallas import tpu as pltpu
from jax.sharding import Mesh
from jax.sharding import PartitionSpec as P

DH = 128
RUN = 64
DOCS = 8
SIZES = (256, 512, 768, 1024, 1152, 1536, 2304)
NEGATIVE = -1e30
Z = ("zh", "zl")


def z_index():
    return lax.axis_index("zh") * 2 + lax.axis_index("zl")


def shift(value, axis, step):
    return lax.ppermute(value, axis, [(i, (i + step) % 4) for i in range(4)])


def swap_cores(value):
    return lax.ppermute(value, "c", [(0, 1), (1, 0)])


def plus(first, second):
    return (first.astype(jnp.float32) + second.astype(jnp.float32)).astype(jnp.bfloat16)


SMEM = pl.BlockSpec(memory_space=pltpu.SMEM)
VMEM = pl.BlockSpec(memory_space=pltpu.VMEM)


def place_kernel(held, pos, *refs):
    blocks, outs = refs[: len(held)], refs[-2:]
    z, x = z_index(), lax.axis_index("x")
    for ref, items in zip(blocks, held):
        rows = ref.shape[0] // len(items)
        runs = rows // RUN
        for n, (dz, dx, which) in enumerate(items):
            group = lax.rem(z + dz, 4) * 4 + lax.rem(x + dx, 4)
            for i in range(runs):
                at = pl.multiple_of(pos[group * runs + i], RUN)
                row = n * rows + i * RUN
                outs[which][pl.ds(at, RUN), :] = ref[row : row + RUN, :]


def place(runs, slots, held, blocks, ordered=None):
    shape = jax.ShapeDtypeStruct((slots, DH), jnp.bfloat16)
    old = list(ordered or ())
    at = 1 + len(blocks)
    return pl.pallas_call(
        functools.partial(place_kernel, held),
        out_shape=[shape, shape],
        in_specs=[SMEM] + [VMEM] * (len(blocks) + len(old)),
        out_specs=[VMEM, VMEM],
        input_output_aliases={at: 0, at + 1: 1} if old else {},
        compiler_params=pltpu.CompilerParams(vmem_limit_bytes=6 * 2**20),
        cost_estimate=pl.CostEstimate(flops=0, bytes_accessed=2 * 2**20, transcendentals=0),
        name="place",
    )(runs, *blocks, *old)


def attend_kernel(pos, q, ks, vs, out):
    z, x = z_index(), lax.axis_index("x")
    heads, slots = out.shape[1] // DH, ks.shape[0]
    runs = out.shape[0] // RUN

    first_length, first_span = slots // RUN, slots // RUN + DOCS
    ends = []
    for d in range(DOCS):
        ends.append(pos[first_length + d] + (ends[-1] if ends else 0))
    starts = [0] + ends[:-1]
    count = (pos.shape[0] - first_span) // 2
    span_list = [(pos[first_span + k], pos[first_span + count + k]) for k in range(count)]

    def interval(at):
        low = jnp.zeros_like(at)
        end = jnp.zeros_like(at)
        for first, last in zip(starts, ends):
            inside = (at >= first) & (at < last)
            low = jnp.where(inside, first, low)
            end = jnp.where(inside, last, end)
        high = at + 1
        for first, last in span_list:
            inside = (at >= first) & (at < last)
            high = jnp.where(inside, jnp.maximum(high, jnp.minimum(last, end)), high)
        return low, high

    scale = math.log2(math.e) / math.sqrt(DH)
    first_run = (z * 4 + x) * runs

    def block(i, _):
        p0 = pos[first_run + i]
        row = pl.multiple_of(i * RUN, RUN)
        low, high = interval(p0 + lax.broadcasted_iota(jnp.int32, (RUN, DH), 0))
        width = high - low
        lanes = lax.broadcasted_iota(jnp.int32, (RUN, DH), 1) - low
        first_low, _ = interval(p0)
        _, last_high = interval(p0 + RUN - 1)
        base = first_low // RUN * RUN
        need = last_high - base

        def work(size, groups):
            start = pl.multiple_of(jnp.minimum(base, slots - size), RUN)
            allowed = []
            for n in range(size // DH):
                t = lanes + (start + n * DH)
                allowed.append((t >= 0) & (t < width))
            per = heads // groups
            columns = [[(g * per + h) * DH for h in range(per)] for g in range(groups)]
            scores, mixed = [], []
            for group in columns:
                queries = jnp.concatenate([q[pl.ds(row, RUN), c : c + DH] for c in group], axis=0)
                s = lax.dot_general(
                    queries,
                    ks[pl.ds(start, size), :],
                    (((1,), (1,)), ((), ())),
                    preferred_element_type=jnp.float32,
                )
                scores.append(
                    [
                        jnp.where(
                            allowed[n][None], s[:, n * DH : (n + 1) * DH].reshape(per, RUN, DH), NEGATIVE
                        ).reshape(per * RUN, DH)
                        for n in range(size // DH)
                    ]
                )
            for parts in scores:
                top = jnp.max(functools.reduce(jnp.maximum, parts), axis=1, keepdims=True) * scale
                expo = [jnp.exp2(part * scale - top) for part in parts]
                total = jnp.sum(functools.reduce(jnp.add, expo), axis=1, keepdims=True)
                weights = jnp.concatenate([e.astype(jnp.bfloat16) for e in expo], axis=1)
                mixed.append((jnp.dot(weights, vs[pl.ds(start, size), :], preferred_element_type=jnp.float32), total))
            for group, (value, total) in zip(columns, mixed):
                value = (value / total).astype(jnp.bfloat16)
                for h, c in enumerate(group):
                    out[pl.ds(row, RUN), c : c + DH] = value[h * RUN : (h + 1) * RUN]

        below = 0
        for size in SIZES:

            @pl.when((need > below) & (need <= size))
            def _():
                work(size, 2 if size <= 1152 else 4)

            below = size
        return 0

    lax.fori_loop(0, runs, block, 0)


def attend(runs, q, ordered):
    rows, width = q.shape
    return pl.pallas_call(
        attend_kernel,
        out_shape=jax.ShapeDtypeStruct((rows, width), jnp.bfloat16),
        in_specs=[SMEM] + [VMEM] * 3,
        out_specs=VMEM,
        compiler_params=pltpu.CompilerParams(vmem_limit_bytes=10 * 2**20),
        cost_estimate=pl.CostEstimate(
            flops=24 * rows * 1024 * width, bytes_accessed=4 * 2**20, transcendentals=rows * 8 * width
        ),
        name="attend",
    )(runs, q, *ordered)


def join_kernel(ranges, *refs):
    row = 0
    for ref, (first, last) in zip(refs, ranges):
        refs[-1][row : row + last - first, :] = ref[first:last, :]
        row += last - first


def join(pieces, ranges):
    rows = sum(last - first for first, last in ranges)
    return pl.pallas_call(
        functools.partial(join_kernel, ranges),
        out_shape=jax.ShapeDtypeStruct((rows, pieces[0].shape[1]), pieces[0].dtype),
        in_specs=[VMEM] * len(pieces),
        out_specs=VMEM,
        compiler_params=pltpu.CompilerParams(vmem_limit_bytes=4 * 2**20),
        cost_estimate=pl.CostEstimate(flops=0, bytes_accessed=2**20, transcendentals=0),
        name="join",
    )(*pieces)


BLOCKS = ((0,), (1,), (2,), (3, 4))


def product(rows, weights, parts):
    total, at = None, 0
    for part in parts:
        depth = weights[part].shape[0]
        share = jnp.dot(rows[:, at : at + depth], weights[part][...], preferred_element_type=jnp.float32)
        total = share if total is None else total + share
        at += depth
    return total.astype(jnp.bfloat16)


def near_kernel(left, right, *refs):
    weights, (keep, send, rows) = refs[:-3], refs[-3:]
    core = lax.axis_index("c")
    for at in range(0, left.shape[0], 2 * RUN):
        rows[core, at : at + 2 * RUN, :] = left[at : at + 2 * RUN, :]
        rows[1 - core, at : at + 2 * RUN, :] = right[at : at + 2 * RUN, :]
    for target, which in ((send, 1), (keep, 0)):
        for n, parts in enumerate(BLOCKS):
            target[n] = product(rows.at[which], weights, parts)


def own_kernel(rows, *refs):
    weights, out = refs[:-1], refs[-1]
    for n, parts in enumerate(BLOCKS):
        out[n] = product(rows, weights, parts)


def far_kernel(upper, lower, own, *refs):
    weights, (keep, send, rows) = refs[:-3], refs[-3:]
    core = lax.axis_index("c")
    half = upper.shape[0]
    rows[:half, :] = upper[...]
    rows[half:, :] = lower[...]

    def fill(target, other):
        other[...] = own[...]
        for n, parts in enumerate(BLOCKS):
            target[n] = product(rows, weights, parts)

    @pl.when(core == 0)
    def _():
        fill(send, keep)

    @pl.when(core == 1)
    def _():
        fill(keep, send)


def project(kernel, pieces, weights):
    depth, width = weights[0].shape
    count = 2 * pieces[0].shape[0] if kernel is far_kernel else pieces[0].shape[0]
    result = jax.ShapeDtypeStruct((len(BLOCKS), count, width), jnp.bfloat16)
    results = 1 if kernel is own_kernel else 2
    scratch = {
        own_kernel: [],
        near_kernel: [pltpu.VMEM((2, count, depth), jnp.bfloat16)],
        far_kernel: [pltpu.VMEM((count, depth), jnp.bfloat16)],
    }
    return pl.pallas_call(
        kernel,
        out_shape=[result] * results,
        in_specs=[VMEM] * (len(pieces) + len(weights)),
        out_specs=[VMEM] * results,
        scratch_shapes=scratch[kernel],
        compiler_params=pltpu.CompilerParams(vmem_limit_bytes=10 * 2**20),
        cost_estimate=pl.CostEstimate(
            flops=4 * count * depth * width * len(BLOCKS), bytes_accessed=4 * 2**20, transcendentals=0
        ),
        name="project",
    )(*pieces, *weights)


def combine_kernel(keep, got, *refs):
    outs, stack = refs[:-1], refs[-1]
    z, y, core = z_index(), lax.axis_index("y"), lax.axis_index("c")
    for block, away in enumerate((0, 3, 1, 2)):
        ahead = lax.rem(away + z - y + 4, 4)
        turn = lax.rem(jnp.where(core == 0, 3 - ahead, ahead + 3), 4)
        stack[turn] = plus(keep[block], got[block])
    for n, out in enumerate(outs):
        out[...] = stack[n]


def combine(keep, got):
    _, rows, width = keep.shape
    result = jax.ShapeDtypeStruct((rows, width), jnp.bfloat16)
    return pl.pallas_call(
        combine_kernel,
        out_shape=[result] * 4,
        in_specs=[VMEM] * 2,
        out_specs=[VMEM] * 4,
        scratch_shapes=[pltpu.VMEM(keep.shape, jnp.bfloat16)],
        compiler_params=pltpu.CompilerParams(vmem_limit_bytes=6 * 2**20),
        cost_estimate=pl.CostEstimate(flops=0, bytes_accessed=3 * 2**20, transcendentals=0),
        name="combine",
    )(keep, got)


def relay(value, axis):
    pairs = [(2 * i + c, 2 * ((i + 1 - 2 * c) % 4) + c) for i in range(4) for c in range(2)]
    return lax.ppermute(value, (axis, "c"), pairs)


def home(value, away, turn):
    pairs = []
    for x in range(4):
        for y in range(4):
            for c in range(2):
                to_y = (y + (1 - 2 * c) * turn) % 4
                pairs.append(((x * 4 + y) * 2 + c, (((x + away[c]) % 4) * 4 + to_y) * 2 + x // 2))
    return lax.ppermute(value, ("x", "y", "c"), pairs)


def sum_shares(turns, away):
    stay = home(turns[3], away, 0)
    passed = relay(turns[0], "y")
    passed = relay(plus(turns[1], passed), "y")
    return stay, home(plus(turns[2], passed), away, 1)


def after(value, *others):
    return lax.optimization_barrier((value, *others))[0]


def halves(left, right, axis):
    half = left.shape[0] // 2
    return (
        shift(join((left,), ((0, half),)), axis, 1),
        shift(join((right,), ((half, 2 * half),)), axis, -1),
    )


def shards(queries, keys, values, positions, lengths, spans, weight):
    x = lax.axis_index("x")
    count, slots = keys.shape[0], positions.shape[0]
    kv = jnp.concatenate([keys, values], axis=0)
    line = [shift(kv, Z, 1), shift(kv, Z, -1), shift(kv, Z, 2)]
    left, right = shift(kv, "x", 1), shift(kv, "x", -1)
    line = jnp.concatenate(line, axis=0)
    line, weight, left, right = lax.optimization_barrier((line, weight, left, right))
    line_left, line_right = shift(line, "x", 1), shift(line, "x", -1)
    weight_left, weight_right = shift(weight, Z, 1), shift(weight, Z, -1)

    runs = positions.reshape(-1, RUN)[:, 0]
    runs = jnp.concatenate([runs, lengths, spans[0], spans[1]])
    line_blocks = [(dz, which) for dz in (3, 1, 2) for which in (0, 1)]

    def at_x(dx, blocks=line_blocks):
        return [(dz, dx, which) for dz, which in blocks]

    here = [(0, 0), (0, 1)]
    ordered = place(runs, slots, (at_x(0, here), at_x(0), at_x(3, here), at_x(1, here)), (kv, line, left, right))
    left2 = shift(join((line_left, left), ((0, 3 * count), (0, count))), "x", 1)
    right2 = shift(join((line_right, right), ((3 * count, 6 * count), (count, 2 * count))), "x", -1)
    ordered = place(runs, slots, (at_x(3), at_x(1)), (line_left, line_right), ordered)
    ordered = place(
        runs,
        slots,
        (at_x(2, line_blocks[:3] + here[:1]), at_x(2, line_blocks[3:] + here[1:])),
        (left2, right2),
        ordered,
    )

    own = attend(runs, queries, ordered)
    rows_left, rows_right = shift(own, "x", 1), shift(own, "x", -1)
    rows_far = halves(rows_left, rows_right, "x")
    weight_far = halves(after(weight_left, own), after(weight_right, own), Z)

    weights = (weight, weight_left, weight_right, *weight_far)
    (own,) = project(own_kernel, (own,), weights)
    rows = (after(rows_left, own), rows_right)
    keep, send = project(near_kernel, rows, weights)
    near = combine(keep, swap_cores(send))
    keep, send = project(far_kernel, (*rows_far, own), weights)
    mixed = combine(keep, swap_cores(send))

    near = plus(*sum_shares(near, (-1, 1)))
    mixed = plus(*sum_shares(mixed, (0, 2)))
    return jnp.where(
        lax.rem(x, 2) == 0,
        jnp.concatenate([mixed, near], axis=1),
        jnp.concatenate([near, mixed], axis=1),
    )


def solution(mesh):
    fine = Mesh(mesh.devices.reshape(2, 2, 4, 4, 2), ("zh", "zl", "x", "y", "c"))
    rows, columns = ("zh", "zl", "x"), ("y", "c")
    return jax.shard_map(
        shards,
        mesh=fine,
        in_specs=(P(rows, columns), P(rows, columns), P(rows, columns), P(), P(), P(), P(columns, rows)),
        out_specs=P(rows, columns),
        check_vma=False,
    )
```

```python
import functools
import math

import jax
import jax.numpy as jnp
from jax import lax
from jax.experimental import pallas as pl
from jax.experimental.pallas import tpu as pltpu
from jax.sharding import Mesh
from jax.sharding import PartitionSpec as P

DH = 128
RUN = 64
DOCS = 8
SIZES = (256, 384, 512, 640, 768, 896, 1024, 1152, 1536, 2304)
NEGATIVE = -1e30
Z = ("zh", "zl")


def z_index():
    return lax.axis_index("zh") * 2 + lax.axis_index("zl")


def shift(value, axis, step):
    return lax.ppermute(value, axis, [(i, (i + step) % 4) for i in range(4)])


def swap_cores(value):
    return lax.ppermute(value, "c", [(0, 1), (1, 0)])


def plus(first, second):
    return (first.astype(jnp.float32) + second.astype(jnp.float32)).astype(jnp.bfloat16)


SMEM = pl.BlockSpec(memory_space=pltpu.SMEM)
VMEM = pl.BlockSpec(memory_space=pltpu.VMEM)


def place_kernel(held, pos, *refs):
    blocks, outs = refs[: len(held)], refs[-2:]
    z, x = z_index(), lax.axis_index("x")
    for ref, items in zip(blocks, held):
        rows = ref.shape[0] // len(items)
        runs = rows // RUN
        for n, (dz, dx, which) in enumerate(items):
            group = lax.rem(z + dz, 4) * 4 + lax.rem(x + dx, 4)
            for i in range(runs):
                at = pl.multiple_of(pos[group * runs + i], RUN)
                row = n * rows + i * RUN
                outs[which][pl.ds(at, RUN), :] = ref[row : row + RUN, :]


def place(runs, slots, held, blocks, ordered=None):
    shape = jax.ShapeDtypeStruct((slots, DH), jnp.bfloat16)
    old = list(ordered or ())
    at = 1 + len(blocks)
    return pl.pallas_call(
        functools.partial(place_kernel, held),
        out_shape=[shape, shape],
        in_specs=[SMEM] + [VMEM] * (len(blocks) + len(old)),
        out_specs=[VMEM, VMEM],
        input_output_aliases={at: 0, at + 1: 1} if old else {},
        compiler_params=pltpu.CompilerParams(vmem_limit_bytes=6 * 2**20),
        cost_estimate=pl.CostEstimate(flops=0, bytes_accessed=2 * 2**20, transcendentals=0),
        name="place",
    )(runs, *blocks, *old)


def attend_kernel(pos, q, ks, vs, out):
    z, x = z_index(), lax.axis_index("x")
    heads, slots = out.shape[1] // DH, ks.shape[0]
    runs = out.shape[0] // RUN

    first_length, first_span = slots // RUN, slots // RUN + DOCS
    ends = []
    for d in range(DOCS):
        ends.append(pos[first_length + d] + (ends[-1] if ends else 0))
    starts = [0] + ends[:-1]
    count = (pos.shape[0] - first_span) // 2
    span_list = [(pos[first_span + k], pos[first_span + count + k]) for k in range(count)]

    def interval(at):
        low = jnp.zeros_like(at)
        end = jnp.zeros_like(at)
        for first, last in zip(starts, ends):
            inside = (at >= first) & (at < last)
            low = jnp.where(inside, first, low)
            end = jnp.where(inside, last, end)
        high = at + 1
        for first, last in span_list:
            inside = (at >= first) & (at < last)
            high = jnp.where(inside, jnp.maximum(high, jnp.minimum(last, end)), high)
        return low, high

    scale = math.log2(math.e) / math.sqrt(DH)
    first_run = (z * 4 + x) * runs

    def block(i, _):
        p0 = pos[first_run + i]
        row = pl.multiple_of(i * RUN, RUN)
        low, high = interval(p0 + lax.broadcasted_iota(jnp.int32, (RUN, DH), 0))
        width = high - low
        lanes = lax.broadcasted_iota(jnp.int32, (RUN, DH), 1) - low
        first_low, _ = interval(p0)
        _, last_high = interval(p0 + RUN - 1)
        base = first_low // RUN * RUN
        need = last_high - base

        def work(size, groups):
            start = pl.multiple_of(jnp.minimum(base, slots - size), RUN)
            allowed = []
            for n in range(size // DH):
                t = lanes + (start + n * DH)
                allowed.append((t >= 0) & (t < width))
            per = heads // groups
            columns = [[(g * per + h) * DH for h in range(per)] for g in range(groups)]
            scores, mixed = [], []
            for group in columns:
                queries = jnp.concatenate([q[pl.ds(row, RUN), c : c + DH] for c in group], axis=0)
                s = lax.dot_general(
                    queries,
                    ks[pl.ds(start, size), :],
                    (((1,), (1,)), ((), ())),
                    preferred_element_type=jnp.float32,
                )
                scores.append(
                    [
                        jnp.where(
                            allowed[n][None], s[:, n * DH : (n + 1) * DH].reshape(per, RUN, DH), NEGATIVE
                        ).reshape(per * RUN, DH)
                        for n in range(size // DH)
                    ]
                )
            for parts in scores:
                top = jnp.max(functools.reduce(jnp.maximum, parts), axis=1, keepdims=True) * scale
                expo = [jnp.exp2(part * scale - top) for part in parts]
                total = jnp.sum(functools.reduce(jnp.add, expo), axis=1, keepdims=True)
                weights = jnp.concatenate([e.astype(jnp.bfloat16) for e in expo], axis=1)
                mixed.append((jnp.dot(weights, vs[pl.ds(start, size), :], preferred_element_type=jnp.float32), total))
            for group, (value, total) in zip(columns, mixed):
                value = (value / total).astype(jnp.bfloat16)
                for h, c in enumerate(group):
                    out[pl.ds(row, RUN), c : c + DH] = value[h * RUN : (h + 1) * RUN]

        below = 0
        for size in SIZES:

            @pl.when((need > below) & (need <= size))
            def _():
                work(size, 2 if size <= 1152 else 4)

            below = size
        return 0

    lax.fori_loop(0, runs, block, 0)


def attend(runs, q, ordered):
    rows, width = q.shape
    return pl.pallas_call(
        attend_kernel,
        out_shape=jax.ShapeDtypeStruct((rows, width), jnp.bfloat16),
        in_specs=[SMEM] + [VMEM] * 3,
        out_specs=VMEM,
        compiler_params=pltpu.CompilerParams(vmem_limit_bytes=10 * 2**20),
        cost_estimate=pl.CostEstimate(
            flops=24 * rows * 1024 * width, bytes_accessed=4 * 2**20, transcendentals=rows * 8 * width
        ),
        name="attend",
    )(runs, q, *ordered)


def far_parts_kernel(cut, line_left, left, line_right, right, upper, lower):
    count = left.shape[0] // 2
    upper[:cut, :] = line_left[:cut, :]
    upper[cut:, :] = left[:count, :]
    lower[:cut, :] = line_right[cut:, :]
    lower[cut:, :] = right[count:, :]


def far_parts(line_left, left, line_right, right):
    cut, count = line_left.shape[0] // 2, left.shape[0] // 2
    half = jax.ShapeDtypeStruct((cut + count, left.shape[1]), left.dtype)
    return pl.pallas_call(
        functools.partial(far_parts_kernel, cut),
        out_shape=[half, half],
        in_specs=[VMEM] * 4,
        out_specs=[VMEM] * 2,
        compiler_params=pltpu.CompilerParams(vmem_limit_bytes=4 * 2**20),
        cost_estimate=pl.CostEstimate(flops=0, bytes_accessed=2**20, transcendentals=0),
        name="far_parts",
    )(line_left, left, line_right, right)


def join_kernel(ranges, *refs):
    row = 0
    for ref, (first, last) in zip(refs, ranges):
        refs[-1][row : row + last - first, :] = ref[first:last, :]
        row += last - first


def join(pieces, ranges):
    rows = sum(last - first for first, last in ranges)
    return pl.pallas_call(
        functools.partial(join_kernel, ranges),
        out_shape=jax.ShapeDtypeStruct((rows, pieces[0].shape[1]), pieces[0].dtype),
        in_specs=[VMEM] * len(pieces),
        out_specs=VMEM,
        compiler_params=pltpu.CompilerParams(vmem_limit_bytes=4 * 2**20),
        cost_estimate=pl.CostEstimate(flops=0, bytes_accessed=2**20, transcendentals=0),
        name="join",
    )(*pieces)


BLOCKS = ((0,), (1,), (2,), (3, 4))


def product(rows, weights, parts):
    total, at = None, 0
    for part in parts:
        depth = weights[part].shape[0]
        share = jnp.dot(rows[:, at : at + depth], weights[part][...], preferred_element_type=jnp.float32)
        total = share if total is None else total + share
        at += depth
    return total.astype(jnp.bfloat16)


def near_kernel(left, right, *refs):
    weights, (keep, send, rows) = refs[:-3], refs[-3:]
    core = lax.axis_index("c")
    for at in range(0, left.shape[0], 2 * RUN):
        rows[core, at : at + 2 * RUN, :] = left[at : at + 2 * RUN, :]
        rows[1 - core, at : at + 2 * RUN, :] = right[at : at + 2 * RUN, :]
    for target, which in ((send, 1), (keep, 0)):
        for n, parts in enumerate(BLOCKS):
            target[n] = product(rows.at[which], weights, parts)


def own_kernel(rows, *refs):
    weights, out = refs[:-1], refs[-1]
    for n, parts in enumerate(BLOCKS):
        out[n] = product(rows, weights, parts)


def far_kernel(upper, lower, own, *refs):
    weights, (keep, send, rows) = refs[:-3], refs[-3:]
    core = lax.axis_index("c")
    half = upper.shape[0]
    rows[:half, :] = upper[...]
    rows[half:, :] = lower[...]

    def fill(target, other):
        other[...] = own[...]
        for n, parts in enumerate(BLOCKS):
            target[n] = product(rows, weights, parts)

    @pl.when(core == 0)
    def _():
        fill(send, keep)

    @pl.when(core == 1)
    def _():
        fill(keep, send)


def project(kernel, pieces, weights):
    depth, width = weights[0].shape
    count = 2 * pieces[0].shape[0] if kernel is far_kernel else pieces[0].shape[0]
    result = jax.ShapeDtypeStruct((len(BLOCKS), count, width), jnp.bfloat16)
    results = 1 if kernel is own_kernel else 2
    scratch = {
        own_kernel: [],
        near_kernel: [pltpu.VMEM((2, count, depth), jnp.bfloat16)],
        far_kernel: [pltpu.VMEM((count, depth), jnp.bfloat16)],
    }
    return pl.pallas_call(
        kernel,
        out_shape=[result] * results,
        in_specs=[VMEM] * (len(pieces) + len(weights)),
        out_specs=[VMEM] * results,
        scratch_shapes=scratch[kernel],
        compiler_params=pltpu.CompilerParams(vmem_limit_bytes=10 * 2**20),
        cost_estimate=pl.CostEstimate(
            flops=4 * count * depth * width * len(BLOCKS), bytes_accessed=4 * 2**20, transcendentals=0
        ),
        name="project",
    )(*pieces, *weights)


def combine_kernel(keep, got, *refs):
    outs, stack = refs[:-1], refs[-1]
    z, y, core = z_index(), lax.axis_index("y"), lax.axis_index("c")
    for block, away in enumerate((0, 3, 1, 2)):
        ahead = lax.rem(away + z - y + 4, 4)
        turn = lax.rem(jnp.where(core == 0, 3 - ahead, ahead + 3), 4)
        stack[turn] = plus(keep[block], got[block])
    for n, out in enumerate(outs):
        out[...] = stack[n]


def combine(keep, got):
    _, rows, width = keep.shape
    result = jax.ShapeDtypeStruct((rows, width), jnp.bfloat16)
    return pl.pallas_call(
        combine_kernel,
        out_shape=[result] * 4,
        in_specs=[VMEM] * 2,
        out_specs=[VMEM] * 4,
        scratch_shapes=[pltpu.VMEM(keep.shape, jnp.bfloat16)],
        compiler_params=pltpu.CompilerParams(vmem_limit_bytes=6 * 2**20),
        cost_estimate=pl.CostEstimate(flops=0, bytes_accessed=3 * 2**20, transcendentals=0),
        name="combine",
    )(keep, got)


def relay(value, axis):
    pairs = [(2 * i + c, 2 * ((i + 1 - 2 * c) % 4) + c) for i in range(4) for c in range(2)]
    return lax.ppermute(value, (axis, "c"), pairs)


def home(value, away, turn):
    pairs = []
    for x in range(4):
        for y in range(4):
            for c in range(2):
                to_y = (y + (1 - 2 * c) * turn) % 4
                pairs.append(((x * 4 + y) * 2 + c, (((x + away[c]) % 4) * 4 + to_y) * 2 + x // 2))
    return lax.ppermute(value, ("x", "y", "c"), pairs)


def sum_shares(turns, away):
    stay = home(turns[3], away, 0)
    passed = relay(turns[0], "y")
    passed = relay(plus(turns[1], passed), "y")
    return stay, home(plus(turns[2], passed), away, 1)


def after(value, *others):
    return lax.optimization_barrier((value, *others))[0]


def halves(left, right, axis):
    half = left.shape[0] // 2
    return (
        shift(join((left,), ((0, half),)), axis, 1),
        shift(join((right,), ((half, 2 * half),)), axis, -1),
    )


def shards(queries, keys, values, positions, lengths, spans, weight):
    x = lax.axis_index("x")
    count, slots = keys.shape[0], positions.shape[0]
    kv = jnp.concatenate([keys, values], axis=0)
    line = [shift(kv, Z, 1), shift(kv, Z, -1), shift(kv, Z, 2)]
    left, right = shift(kv, "x", 1), shift(kv, "x", -1)
    line = jnp.concatenate(line, axis=0)
    line, weight, left, right = lax.optimization_barrier((line, weight, left, right))
    line_left, line_right = shift(line, "x", 1), shift(line, "x", -1)
    weight_left, weight_right = shift(weight, Z, 1), shift(weight, Z, -1)

    runs = positions.reshape(-1, RUN)[:, 0]
    runs = jnp.concatenate([runs, lengths, spans[0], spans[1]])
    line_blocks = [(dz, which) for dz in (3, 1, 2) for which in (0, 1)]

    def at_x(dx, blocks=line_blocks):
        return [(dz, dx, which) for dz, which in blocks]

    here = [(0, 0), (0, 1)]
    ordered = place(runs, slots, (at_x(0, here), at_x(0), at_x(3, here), at_x(1, here)), (kv, line, left, right))
    left2, right2 = far_parts(line_left, left, line_right, right)
    left2, right2 = shift(left2, "x", 1), shift(right2, "x", -1)
    ordered = place(runs, slots, (at_x(3), at_x(1)), (line_left, line_right), ordered)
    ordered = place(
        runs,
        slots,
        (at_x(2, line_blocks[:3] + here[:1]), at_x(2, line_blocks[3:] + here[1:])),
        (left2, right2),
        ordered,
    )

    own = attend(runs, queries, ordered)
    rows_left, rows_right = shift(own, "x", 1), shift(own, "x", -1)
    rows_far = halves(rows_left, rows_right, "x")
    weight_far = halves(after(weight_left, own), after(weight_right, own), Z)

    weights = (weight, weight_left, weight_right, *weight_far)
    (own,) = project(own_kernel, (own,), weights)
    rows = (after(rows_left, own), rows_right)
    keep, send = project(near_kernel, rows, weights)
    near = combine(keep, swap_cores(send))
    keep, send = project(far_kernel, (*rows_far, own), weights)
    mixed = combine(keep, swap_cores(send))

    near = plus(*sum_shares(near, (-1, 1)))
    mixed = plus(*sum_shares(mixed, (0, 2)))
    return jnp.where(
        lax.rem(x, 2) == 0,
        jnp.concatenate([mixed, near], axis=1),
        jnp.concatenate([near, mixed], axis=1),
    )


def solution(mesh):
    fine = Mesh(mesh.devices.reshape(2, 2, 4, 4, 2), ("zh", "zl", "x", "y", "c"))
    rows, columns = ("zh", "zl", "x"), ("y", "c")
    return jax.shard_map(
        shards,
        mesh=fine,
        in_specs=(P(rows, columns), P(rows, columns), P(rows, columns), P(), P(), P(), P(columns, rows)),
        out_specs=P(rows, columns),
        check_vma=False,
    )
```

```python
import functools
import math

import jax
import jax.numpy as jnp
from jax import lax
from jax.experimental import pallas as pl
from jax.experimental.pallas import tpu as pltpu
from jax.sharding import Mesh
from jax.sharding import PartitionSpec as P

DH = 128
RUN = 64
DOCS = 8
SIZES = (256, 384, 512, 640, 768, 896, 1024, 1152, 1536, 2304)
NEGATIVE = -1e30
Z = ("zh", "zl")


def z_index():
    return lax.axis_index("zh") * 2 + lax.axis_index("zl")


def shift(value, axis, step):
    return lax.ppermute(value, axis, [(i, (i + step) % 4) for i in range(4)])


def swap_cores(value):
    return lax.ppermute(value, "c", [(0, 1), (1, 0)])


def plus(first, second):
    return (first.astype(jnp.float32) + second.astype(jnp.float32)).astype(jnp.bfloat16)


SMEM = pl.BlockSpec(memory_space=pltpu.SMEM)
VMEM = pl.BlockSpec(memory_space=pltpu.VMEM)


def place_kernel(held, pos, *refs):
    blocks, outs = refs[: len(held)], refs[-2:]
    z, x = z_index(), lax.axis_index("x")
    for ref, items in zip(blocks, held):
        rows = ref.shape[0] // len(items)
        runs = rows // RUN
        for n, (dz, dx, which) in enumerate(items):
            group = lax.rem(z + dz, 4) * 4 + lax.rem(x + dx, 4)
            for i in range(runs):
                at = pl.multiple_of(pos[group * runs + i], RUN)
                row = n * rows + i * RUN
                outs[which][pl.ds(at, RUN), :] = ref[row : row + RUN, :]


def place(runs, slots, held, blocks, ordered=None):
    shape = jax.ShapeDtypeStruct((slots, DH), jnp.bfloat16)
    old = list(ordered or ())
    at = 1 + len(blocks)
    return pl.pallas_call(
        functools.partial(place_kernel, held),
        out_shape=[shape, shape],
        in_specs=[SMEM] + [VMEM] * (len(blocks) + len(old)),
        out_specs=[VMEM, VMEM],
        input_output_aliases={at: 0, at + 1: 1} if old else {},
        compiler_params=pltpu.CompilerParams(vmem_limit_bytes=6 * 2**20),
        cost_estimate=pl.CostEstimate(flops=0, bytes_accessed=2 * 2**20, transcendentals=0),
        name="place",
    )(runs, *blocks, *old)


def attend_kernel(pos, q, ks, vs, out):
    z, x = z_index(), lax.axis_index("x")
    heads, slots = out.shape[1] // DH, ks.shape[0]
    runs = out.shape[0] // RUN

    first_length, first_span = slots // RUN, slots // RUN + DOCS
    ends = []
    for d in range(DOCS):
        ends.append(pos[first_length + d] + (ends[-1] if ends else 0))
    starts = [0] + ends[:-1]
    count = (pos.shape[0] - first_span) // 2
    span_list = [(pos[first_span + k], pos[first_span + count + k]) for k in range(count)]

    def interval(at):
        low = jnp.zeros_like(at)
        end = jnp.zeros_like(at)
        for first, last in zip(starts, ends):
            inside = (at >= first) & (at < last)
            low = jnp.where(inside, first, low)
            end = jnp.where(inside, last, end)
        high = at + 1
        for first, last in span_list:
            inside = (at >= first) & (at < last)
            high = jnp.where(inside, jnp.maximum(high, jnp.minimum(last, end)), high)
        return low, high

    scale = math.log2(math.e) / math.sqrt(DH)
    first_run = (z * 4 + x) * runs

    def block(i, _):
        p0 = pos[first_run + i]
        row = pl.multiple_of(i * RUN, RUN)
        low, high = interval(p0 + lax.broadcasted_iota(jnp.int32, (RUN, DH), 0))
        width = high - low
        lanes = lax.broadcasted_iota(jnp.int32, (RUN, DH), 1) - low
        first_low, _ = interval(p0)
        _, last_high = interval(p0 + RUN - 1)
        base = first_low // RUN * RUN
        need = last_high - base

        def work(size, groups):
            start = pl.multiple_of(jnp.minimum(base, slots - size), RUN)
            allowed = []
            for n in range(size // DH):
                t = lanes + (start + n * DH)
                allowed.append((t >= 0) & (t < width))
            per = heads // groups
            columns = [[(g * per + h) * DH for h in range(per)] for g in range(groups)]
            scores, mixed = [], []
            for group in columns:
                queries = jnp.concatenate([q[pl.ds(row, RUN), c : c + DH] for c in group], axis=0)
                s = lax.dot_general(
                    queries,
                    ks[pl.ds(start, size), :],
                    (((1,), (1,)), ((), ())),
                    preferred_element_type=jnp.float32,
                )
                scores.append(
                    [
                        jnp.where(
                            allowed[n][None], s[:, n * DH : (n + 1) * DH].reshape(per, RUN, DH), NEGATIVE
                        ).reshape(per * RUN, DH)
                        for n in range(size // DH)
                    ]
                )
            for parts in scores:
                top = jnp.max(functools.reduce(jnp.maximum, parts), axis=1, keepdims=True) * scale
                expo = [jnp.exp2(part * scale - top) for part in parts]
                total = jnp.sum(functools.reduce(jnp.add, expo), axis=1, keepdims=True)
                weights = jnp.concatenate([e.astype(jnp.bfloat16) for e in expo], axis=1)
                mixed.append((jnp.dot(weights, vs[pl.ds(start, size), :], preferred_element_type=jnp.float32), total))
            for group, (value, total) in zip(columns, mixed):
                value = (value / total).astype(jnp.bfloat16)
                for h, c in enumerate(group):
                    out[pl.ds(row, RUN), c : c + DH] = value[h * RUN : (h + 1) * RUN]

        below = 0
        for size in SIZES:

            @pl.when((need > below) & (need <= size))
            def _():
                work(size, 2 if size <= 1152 else 4)

            below = size
        return 0

    lax.fori_loop(0, runs, block, 0)


def attend(runs, q, ordered):
    rows, width = q.shape
    return pl.pallas_call(
        attend_kernel,
        out_shape=jax.ShapeDtypeStruct((rows, width), jnp.bfloat16),
        in_specs=[SMEM] + [VMEM] * 3,
        out_specs=VMEM,
        compiler_params=pltpu.CompilerParams(vmem_limit_bytes=10 * 2**20),
        cost_estimate=pl.CostEstimate(
            flops=24 * rows * 1024 * width, bytes_accessed=4 * 2**20, transcendentals=rows * 8 * width
        ),
        name="attend",
    )(runs, q, *ordered)


def far_parts_kernel(cut, line_left, left, line_right, right, upper, lower):
    count = left.shape[0] // 2
    upper[:cut, :] = line_left[:cut, :]
    upper[cut:, :] = left[:count, :]
    lower[:cut, :] = line_right[cut:, :]
    lower[cut:, :] = right[count:, :]


def far_parts(line_left, left, line_right, right):
    cut, count = line_left.shape[0] // 2, left.shape[0] // 2
    half = jax.ShapeDtypeStruct((cut + count, left.shape[1]), left.dtype)
    return pl.pallas_call(
        functools.partial(far_parts_kernel, cut),
        out_shape=[half, half],
        in_specs=[VMEM] * 4,
        out_specs=[VMEM] * 2,
        compiler_params=pltpu.CompilerParams(vmem_limit_bytes=4 * 2**20),
        cost_estimate=pl.CostEstimate(flops=0, bytes_accessed=2**20, transcendentals=0),
        name="far_parts",
    )(line_left, left, line_right, right)


def join_kernel(ranges, *refs):
    row = 0
    for ref, (first, last) in zip(refs, ranges):
        refs[-1][row : row + last - first, :] = ref[first:last, :]
        row += last - first


def join(pieces, ranges):
    rows = sum(last - first for first, last in ranges)
    return pl.pallas_call(
        functools.partial(join_kernel, ranges),
        out_shape=jax.ShapeDtypeStruct((rows, pieces[0].shape[1]), pieces[0].dtype),
        in_specs=[VMEM] * len(pieces),
        out_specs=VMEM,
        compiler_params=pltpu.CompilerParams(vmem_limit_bytes=4 * 2**20),
        cost_estimate=pl.CostEstimate(flops=0, bytes_accessed=2**20, transcendentals=0),
        name="join",
    )(*pieces)


BLOCKS = ((0,), (1,), (2,), (3, 4))


def product(rows, weights, parts):
    total, at = None, 0
    for part in parts:
        depth = weights[part].shape[0]
        share = jnp.dot(rows[:, at : at + depth], weights[part][...], preferred_element_type=jnp.float32)
        total = share if total is None else total + share
        at += depth
    return total.astype(jnp.bfloat16)


def near_kernel(left, right, *refs):
    weights, (keep, send, rows) = refs[:-3], refs[-3:]
    core = lax.axis_index("c")
    for at in range(0, left.shape[0], 2 * RUN):
        rows[core, at : at + 2 * RUN, :] = left[at : at + 2 * RUN, :]
        rows[1 - core, at : at + 2 * RUN, :] = right[at : at + 2 * RUN, :]
    for target, which in ((send, 1), (keep, 0)):
        for n, parts in enumerate(BLOCKS):
            target[n] = product(rows.at[which], weights, parts)


def own_kernel(rows, *refs):
    weights, out = refs[:-1], refs[-1]
    for n, parts in enumerate(BLOCKS):
        out[n] = product(rows, weights, parts)


def far_kernel(upper, lower, own, *refs):
    weights, (keep, send, rows) = refs[:-3], refs[-3:]
    core = lax.axis_index("c")
    half = upper.shape[0]
    rows[:half, :] = upper[...]
    rows[half:, :] = lower[...]

    def fill(target, other):
        other[...] = own[...]
        for n, parts in enumerate(BLOCKS):
            target[n] = product(rows, weights, parts)

    @pl.when(core == 0)
    def _():
        fill(send, keep)

    @pl.when(core == 1)
    def _():
        fill(keep, send)


def project(kernel, pieces, weights):
    depth, width = weights[0].shape
    count = 2 * pieces[0].shape[0] if kernel is far_kernel else pieces[0].shape[0]
    result = jax.ShapeDtypeStruct((len(BLOCKS), count, width), jnp.bfloat16)
    results = 1 if kernel is own_kernel else 2
    scratch = {
        own_kernel: [],
        near_kernel: [pltpu.VMEM((2, count, depth), jnp.bfloat16)],
        far_kernel: [pltpu.VMEM((count, depth), jnp.bfloat16)],
    }
    return pl.pallas_call(
        kernel,
        out_shape=[result] * results,
        in_specs=[VMEM] * (len(pieces) + len(weights)),
        out_specs=[VMEM] * results,
        scratch_shapes=scratch[kernel],
        compiler_params=pltpu.CompilerParams(vmem_limit_bytes=10 * 2**20),
        cost_estimate=pl.CostEstimate(
            flops=4 * count * depth * width * len(BLOCKS), bytes_accessed=4 * 2**20, transcendentals=0
        ),
        name="project",
    )(*pieces, *weights)


def combine_kernel(keep, got, *refs):
    outs, stack = refs[:-1], refs[-1]
    z, y, core = z_index(), lax.axis_index("y"), lax.axis_index("c")
    for block, away in enumerate((0, 3, 1, 2)):
        ahead = lax.rem(away + z - y + 4, 4)
        turn = lax.rem(jnp.where(core == 0, 3 - ahead, ahead + 3), 4)
        stack[turn] = plus(keep[block], got[block])
    for n, out in enumerate(outs):
        out[...] = stack[n]


def combine(keep, got):
    _, rows, width = keep.shape
    result = jax.ShapeDtypeStruct((rows, width), jnp.bfloat16)
    return pl.pallas_call(
        combine_kernel,
        out_shape=[result] * 4,
        in_specs=[VMEM] * 2,
        out_specs=[VMEM] * 4,
        scratch_shapes=[pltpu.VMEM(keep.shape, jnp.bfloat16)],
        compiler_params=pltpu.CompilerParams(vmem_limit_bytes=6 * 2**20),
        cost_estimate=pl.CostEstimate(flops=0, bytes_accessed=3 * 2**20, transcendentals=0),
        name="combine",
    )(keep, got)


def finish_kernel(near_stay, near_passed, mixed_stay, mixed_passed, out):
    width = near_stay.shape[1]
    odd = lax.rem(lax.axis_index("x"), 2)
    near_at = pl.multiple_of((1 - odd) * width, width)
    mixed_at = pl.multiple_of(odd * width, width)
    out[:, pl.ds(near_at, width)] = plus(near_stay[...], near_passed[...])
    out[:, pl.ds(mixed_at, width)] = plus(mixed_stay[...], mixed_passed[...])


def finish(*shares):
    rows, width = shares[0].shape
    return pl.pallas_call(
        finish_kernel,
        out_shape=jax.ShapeDtypeStruct((rows, 2 * width), jnp.bfloat16),
        in_specs=[VMEM] * 4,
        out_specs=VMEM,
        compiler_params=pltpu.CompilerParams(vmem_limit_bytes=6 * 2**20),
        cost_estimate=pl.CostEstimate(flops=0, bytes_accessed=2 * 2**20, transcendentals=0),
        name="finish",
    )(*shares)


def relay(value, axis):
    pairs = [(2 * i + c, 2 * ((i + 1 - 2 * c) % 4) + c) for i in range(4) for c in range(2)]
    return lax.ppermute(value, (axis, "c"), pairs)


def home(value, away, turn):
    pairs = []
    for x in range(4):
        for y in range(4):
            for c in range(2):
                to_y = (y + (1 - 2 * c) * turn) % 4
                pairs.append(((x * 4 + y) * 2 + c, (((x + away[c]) % 4) * 4 + to_y) * 2 + x // 2))
    return lax.ppermute(value, ("x", "y", "c"), pairs)


def sum_shares(turns, away):
    stay = home(turns[3], away, 0)
    passed = relay(turns[0], "y")
    passed = relay(plus(turns[1], passed), "y")
    return stay, home(plus(turns[2], passed), away, 1)


def after(value, *others):
    return lax.optimization_barrier((value, *others))[0]


def halves(left, right, axis):
    half = left.shape[0] // 2
    return (
        shift(join((left,), ((0, half),)), axis, 1),
        shift(join((right,), ((half, 2 * half),)), axis, -1),
    )


def shards(queries, keys, values, positions, lengths, spans, weight):
    count, slots = keys.shape[0], positions.shape[0]
    kv = jnp.concatenate([keys, values], axis=0)
    line = [shift(kv, Z, 1), shift(kv, Z, -1), shift(kv, Z, 2)]
    left, right = shift(kv, "x", 1), shift(kv, "x", -1)
    line = jnp.concatenate(line, axis=0)
    line, weight, left, right = lax.optimization_barrier((line, weight, left, right))
    line_left, line_right = shift(line, "x", 1), shift(line, "x", -1)
    weight_left, weight_right = shift(weight, Z, 1), shift(weight, Z, -1)

    runs = positions.reshape(-1, RUN)[:, 0]
    runs = jnp.concatenate([runs, lengths, spans[0], spans[1]])
    line_blocks = [(dz, which) for dz in (3, 1, 2) for which in (0, 1)]

    def at_x(dx, blocks=line_blocks):
        return [(dz, dx, which) for dz, which in blocks]

    here = [(0, 0), (0, 1)]
    ordered = place(runs, slots, (at_x(0, here), at_x(0), at_x(3, here), at_x(1, here)), (kv, line, left, right))
    left2, right2 = far_parts(line_left, left, line_right, right)
    left2, right2 = shift(left2, "x", 1), shift(right2, "x", -1)
    ordered = place(runs, slots, (at_x(3), at_x(1)), (line_left, line_right), ordered)
    ordered = place(
        runs,
        slots,
        (at_x(2, line_blocks[:3] + here[:1]), at_x(2, line_blocks[3:] + here[1:])),
        (left2, right2),
        ordered,
    )

    own = attend(runs, queries, ordered)
    rows_left, rows_right = shift(own, "x", 1), shift(own, "x", -1)
    rows_far = halves(rows_left, rows_right, "x")
    weight_far = halves(after(weight_left, own), after(weight_right, own), Z)

    weights = (weight, weight_left, weight_right, *weight_far)
    (own,) = project(own_kernel, (own,), weights)
    rows = (after(rows_left, own), rows_right)
    keep, send = project(near_kernel, rows, weights)
    near = combine(keep, swap_cores(send))
    keep, send = project(far_kernel, (*rows_far, own), weights)
    mixed = combine(keep, swap_cores(send))

    return finish(*sum_shares(near, (-1, 1)), *sum_shares(mixed, (0, 2)))


def solution(mesh):
    fine = Mesh(mesh.devices.reshape(2, 2, 4, 4, 2), ("zh", "zl", "x", "y", "c"))
    rows, columns = ("zh", "zl", "x"), ("y", "c")
    return jax.shard_map(
        shards,
        mesh=fine,
        in_specs=(P(rows, columns), P(rows, columns), P(rows, columns), P(), P(), P(), P(columns, rows)),
        out_specs=P(rows, columns),
        check_vma=False,
    )
```
